32 devices in a mesh: dp: 8 (over z, x), tensor: 4 (over y, core).
Axes of the slice: x: 2, y: 2, z: 4, core: 2. Of those that a mesh axis runs over, the one named last changes fastest.
Arguments:
- tokens: bfloat16 [13312, 768], P(('dp', 'tensor')), may hold values from -6 to 6
- out_grad: bfloat16 [13312, 768], P(('dp', 'tensor')), may hold values from -6 to 6
- image_lengths: int32 [16, 4], P('dp'), may hold values from 0 to 576, as said below
- norm1_gain: float32 [2, 768], replicated, may hold values from 0.5 to 1.5
- norm1_bias: float32 [2, 768], replicated, may hold values from -3 to 3
- qkv_weight: bfloat16 [2, 3, 768, 768], P(None, None, None, 'tensor'), may hold values from -0.21875 to 0.21875
- qkv_bias: float32 [2, 3, 768], P(None, None, 'tensor'), may hold values from -3 to 3
- rope_freqs: float32 [2, 2, 384], P(None, None, 'tensor'), may hold values from -1 to 1
- out_weight: bfloat16 [2, 768, 768], P(None, 'tensor'), may hold values from -1.75 to 1.75
- out_bias: float32 [2, 768], replicated, may hold values from -3 to 3
- norm2_gain: float32 [2, 768], replicated, may hold values from 0.5 to 1.5
- norm2_bias: float32 [2, 768], replicated, may hold values from -3 to 3
- up_weight: bfloat16 [2, 768, 3072], P(None, None, 'tensor'), may hold values from -0.21875 to 0.21875
- up_bias: float32 [2, 3072], P(None, 'tensor'), may hold values from -3 to 3
- down_weight: bfloat16 [2, 3072, 768], P(None, 'tensor'), may hold values from -0.109375 to 0.109375
- down_bias: float32 [2, 768], replicated, may hold values from -3 to 3
Outputs:
- activations: bfloat16 [13312, 768], P(('dp', 'tensor'))
- input_grad: float32 [13312, 768], P(('dp', 'tensor'))
- norm1_gain_grad: float32 [2, 768], replicated
- norm1_bias_grad: float32 [2, 768], replicated
- qkv_weight_grad: float32 [2, 3, 768, 768], P(None, None, None, 'tensor')
- qkv_bias_grad: float32 [2, 3, 768], P(None, None, 'tensor')
- rope_freqs_grad: float32 [2, 2, 384], P(None, None, 'tensor')
- out_weight_grad: float32 [2, 768, 768], P(None, 'tensor')
- out_bias_grad: float32 [2, 768], replicated
- norm2_gain_grad: float32 [2, 768], replicated
- norm2_bias_grad: float32 [2, 768], replicated
- up_weight_grad: float32 [2, 768, 3072], P(None, None, 'tensor')
- up_bias_grad: float32 [2, 3072], P(None, 'tensor')
- down_weight_grad: float32 [2, 3072, 768], P(None, 'tensor')
- down_bias_grad: float32 [2, 768], replicated
The draws below stay inside these ranges and needn't reach their ends.
Inputs may be any that keep to these rules, and one draw needn't show every extreme that they name: `image_lengths`: in each row the nonzero lengths come first, each 196, 400 or 576; the first is never zero; a row sums to at most 832.
All inputs are finite; a program needn't handle non-finite values.
Results may differ from the reference program's by a relative error of at most 0.024.
Values may be sent and summed in bfloat16 or wider, within the bound.
No kernel may reach another device: no remote copies, remote signals or barrier semaphores. Data moves between devices by JAX's collectives and lax.ppermute only.
A program may use at most 192 MiB of HBM per device.

```python
import jax
import jax.numpy as jnp
from jax import lax

D = 768
HEADS = 12
HEAD_DIM = 64
FF = 3072
LEN = 832
SIDE_S = 14
SIDE_M = 20
SIDE_L = 24
MAX_IMAGES = 4
LAYERS = 2
SEQS = 16
TOKENS = 13312


def draw_image_lengths(key, part):
    key = jax.random.fold_in(key, 7)
    picked = jax.random.randint(key, (SEQS, MAX_IMAGES), 0, 3)
    picked = picked.at[0, 0].set(2).at[0, 1].set(2)
    image_sides = jnp.where(picked == 0, SIDE_S, jnp.where(picked == 1, SIDE_M, SIDE_L)).astype(jnp.int32)
    image_sizes = image_sides * image_sides
    running = jnp.cumsum(image_sizes, axis=1).astype(jnp.int32)
    return jnp.where(running <= LEN, image_sizes, 0).astype(jnp.int32)


def block_levels(rng, shape, shards, low, largest):
    factor_of, own = 1.0, jax.random.fold_in(rng, 6)
    for axis_at, shards_of in shards:
        draws = jnp.exp(jax.random.uniform(jax.random.fold_in(own, axis_at), (shards_of,), jnp.float32, low / len(shards), largest / len(shards)))
        factor_of = factor_of * jnp.repeat(draws, shape[axis_at] // shards_of).reshape([-1 if axis == axis_at else 1 for axis in range(len(shape))])
    return factor_of


def scatter_about(rng, dims, deviation, limit, shards=(), held_as=jnp.bfloat16):
    level = block_levels(rng, dims, shards, -0.22, 0.18) if shards else 1.0
    array = jax.random.normal(rng, dims, jnp.float32) * deviation * level
    return jnp.minimum(jnp.maximum(array, -limit), limit).astype(held_as)


def setup_inputs(seed: int = 0) -> dict:
    streams_of = jax.random.split(jax.random.key(seed), 17)
    return {
        "tokens": scatter_about(streams_of[0], (TOKENS, D), 1.0, 6.0, ((0, 32),)),
        "out_grad": scatter_about(streams_of[1], (TOKENS, D), 1.0, 6.0, ((0, 32),)),
        "image_lengths": draw_image_lengths(jax.random.fold_in(streams_of[16], 71), 0),
        "norm1_gain": jnp.clip(1.0 + 0.1 * jax.random.normal(streams_of[3], (LAYERS, D), jnp.float32), 0.5, 1.5),
        "norm1_bias": scatter_about(streams_of[4], (LAYERS, D), 0.3, 3.0, (), jnp.float32),
        "qkv_weight": scatter_about(streams_of[5], (LAYERS, 3, D, D), D ** -0.5, 0.21875, ((3, 4),)),
        "qkv_bias": scatter_about(streams_of[6], (LAYERS, 3, D), 0.3, 3.0, ((2, 4),), jnp.float32),
        "rope_freqs": jnp.clip(jax.random.uniform(streams_of[7], (LAYERS, 2, D // 2), jnp.float32, -1.0, 1.0) * block_levels(streams_of[7], (LAYERS, 2, D // 2), ((2, 4),), -0.4, 0.0), -1.0, 1.0),
        "out_weight": scatter_about(streams_of[8], (LAYERS, D, D), (D // 64) ** -0.5, 1.75, ((1, 4),)),
        "out_bias": scatter_about(streams_of[9], (LAYERS, D), 0.3, 3.0, (), jnp.float32),
        "norm2_gain": jnp.clip(1.0 + 0.1 * jax.random.normal(streams_of[10], (LAYERS, D), jnp.float32), 0.5, 1.5),
        "norm2_bias": scatter_about(streams_of[11], (LAYERS, D), 0.3, 3.0, (), jnp.float32),
        "up_weight": scatter_about(streams_of[12], (LAYERS, D, FF), D ** -0.5, 0.21875, ((2, 4),)),
        "up_bias": scatter_about(streams_of[13], (LAYERS, FF), 0.3, 3.0, ((1, 4),), jnp.float32),
        "down_weight": scatter_about(streams_of[14], (LAYERS, FF, D), FF ** -0.5, 0.109375, ((1, 4),)),
        "down_bias": scatter_about(streams_of[15], (LAYERS, D), 0.3, 3.0, (), jnp.float32),
    }


EPS = 1e-06
NEGATIVE = -1000000000.0
PRECISE = lax.Precision.HIGHEST

@jax.custom_vjp
def low(v):
    return lax.optimization_barrier(v.astype(jnp.bfloat16)).astype(jnp.float32)

@jax.custom_vjp
def low_back(v):
    return v

def low_keep(v):
    return (low(v), None)

def low_pass(kept, grad):
    return (grad,)

def back_keep(v):
    return (v, None)

def back_low(kept, grad):
    return (low(grad),)
low.defvjp(low_keep, low_pass)
low_back.defvjp(back_keep, back_low)

def normalize(values, gain, shift):
    average = lax.optimization_barrier(jnp.mean(values, axis=-1, keepdims=True))
    centred = values - average
    variance = lax.optimization_barrier(jnp.mean(centred * centred, axis=-1, keepdims=True))
    return centred * lax.rsqrt(variance + EPS) * gain + shift

def places(lengths):
    lengths = lengths.astype(jnp.int32)
    image_ends = jnp.cumsum(lengths, axis=1).astype(jnp.int32)
    image_starts = image_ends - lengths
    position = jnp.arange(LEN, dtype=jnp.int32)
    segment = lax.optimization_barrier(jnp.sum((position[None, :, None] >= image_ends[:, None, :]).astype(jnp.int32), axis=2)).astype(jnp.int32)
    belongs = segment[:, :, None] == jnp.arange(MAX_IMAGES, dtype=jnp.int32)[None, None, :]
    begin_at = lax.optimization_barrier(jnp.sum(jnp.where(belongs, image_starts[:, None, :], 0), axis=2)).astype(jnp.int32)
    image_size = lax.optimization_barrier(jnp.sum(jnp.where(belongs, lengths[:, None, :], 0), axis=2)).astype(jnp.int32)
    image_side = jnp.where(image_size == SIDE_S * SIDE_S, SIDE_S, jnp.where(image_size == SIDE_M * SIDE_M, SIDE_M, SIDE_L)).astype(jnp.int32)
    offset = position[None, :] - begin_at
    inside = segment < MAX_IMAGES
    row_at = jnp.where(inside, offset // image_side, 0).astype(jnp.int32)
    column_at = jnp.where(inside, offset % image_side, 0).astype(jnp.int32)
    return (segment, row_at, column_at)

def rotate(values, freqs, row_at, column_at):
    half_dim = values.shape[-1] // 2
    freq_table = freqs.reshape(2, -1, half_dim)
    angles = row_at.astype(jnp.float32)[..., None, None] * freq_table[0] + column_at.astype(jnp.float32)[..., None, None] * freq_table[1]
    cosine = jnp.cos(angles)
    sine_part = jnp.sin(angles)
    first_half = values[..., :half_dim]
    second_half = values[..., half_dim:]
    return jnp.concatenate([first_half * cosine - second_half * sine_part, first_half * sine_part + second_half * cosine], axis=-1)

def residual_block(values, layer_weights, segment, row_at, column_at):
    norm1_gain, norm1_bias, qkv_weight, qkv_bias, rope_freqs, out_weight, out_bias, norm2_gain, norm2_bias, up_weight, up_bias, down_weight, down_bias = layer_weights
    normed = low(normalize(values, norm1_gain, norm1_bias))
    projected = jnp.einsum('td,kde->kte', normed, qkv_weight, precision=PRECISE) + qkv_bias[:, None, :]
    head_shape = (SEQS, LEN, HEADS, HEAD_DIM)
    query_part = low_back(projected[0]).reshape(head_shape)
    key_part = low_back(projected[1]).reshape(head_shape)
    value_part = low(low_back(projected[2])).reshape(head_shape)
    scaling = HEAD_DIM ** (-0.5)

    def one_sequence(pieces):
        query_seq, key_seq, value_seq, segment_seq, row_seq, column_seq = pieces
        turned_q = low(rotate(query_seq, rope_freqs, row_seq, column_seq))
        turned_k = low(rotate(key_seq, rope_freqs, row_seq, column_seq))
        scores = low_back(jnp.einsum('qhe,khe->hqk', turned_q, turned_k, precision=PRECISE) * scaling)
        allowed = segment_seq[:, None] == segment_seq[None, :]
        scores = jnp.where(allowed[None], scores, NEGATIVE)
        attn_probs = low(jax.nn.softmax(scores, axis=-1))
        return jnp.einsum('hqk,khe->qhe', attn_probs, value_seq, precision=PRECISE)
    mixed_heads = lax.map(jax.checkpoint(one_sequence), (query_part, key_part, value_part, segment, row_at, column_at))
    mixed_heads = low(low_back(mixed_heads.reshape(TOKENS, D)))
    middle = values + low_back(jnp.dot(mixed_heads, out_weight, precision=PRECISE) + out_bias)
    normed_mlp = low(normalize(middle, norm2_gain, norm2_bias))
    pre_gelu = low_back(jnp.dot(normed_mlp, up_weight, precision=PRECISE) + up_bias)
    active = low(jax.nn.gelu(pre_gelu, approximate=False))
    return middle + low_back(jnp.dot(active, down_weight, precision=PRECISE) + down_bias)

def forward(values, weights, segment, row_at, column_at):
    for layer_at in range(LAYERS):
        values = residual_block(values, tuple((weight[layer_at] for weight in weights)), segment, row_at, column_at)
    return values

def reference(tokens, out_grad, image_lengths, norm1_gain, norm1_bias, qkv_weight, qkv_bias, rope_freqs, out_weight, out_bias, norm2_gain, norm2_bias, up_weight, up_bias, down_weight, down_bias):
    segment, row_at, column_at = places(image_lengths)
    weights = tuple((weight.astype(jnp.float32) for weight in (norm1_gain, norm1_bias, qkv_weight, qkv_bias, rope_freqs, out_weight, out_bias, norm2_gain, norm2_bias, up_weight, up_bias, down_weight, down_bias)))

    def whole_model(values, params):
        return forward(values, params, segment, row_at, column_at)
    outputs, pullback = jax.vjp(whole_model, tokens.astype(jnp.float32), weights)
    input_grad, weight_grads = pullback(out_grad.astype(jnp.float32))
    return (outputs.astype(jnp.bfloat16), input_grad, weight_grads[0], weight_grads[1], weight_grads[2], weight_grads[3], weight_grads[4], weight_grads[5], weight_grads[6], weight_grads[7], weight_grads[8], weight_grads[9], weight_grads[10], weight_grads[11], weight_grads[12])
```

```python
from functools import partial

import jax
import jax.numpy as jnp
from jax import lax
from jax.sharding import PartitionSpec as P

HEAD_DIM = 64
LEN = 832
SIDE_S = 14
SIDE_M = 20
SIDE_L = 24
MAX_IMAGES = 4
LAYERS = 2

EPS = 1e-06
NEGATIVE = -1000000000.0
BF = jnp.bfloat16
F32 = jnp.float32

CORE = [(0, 1), (1, 0), (2, 3), (3, 2)]
ACROSS = [(0, 2), (2, 0), (1, 3), (3, 1)]


def over_core(values):
    return lax.ppermute(values, "tensor", CORE)


def over_y(values):
    return lax.ppermute(values, "tensor", ACROSS)


def over_bit(values, bit):
    size = lax.axis_size("dp")
    return lax.ppermute(values, "dp", [(at, at ^ (1 << bit)) for at in range(size)])


def quarters(own):
    first = over_core(own)
    second = over_y(own)
    third = over_core(second)
    return (own, first, second, third)


def places_at(lengths, position):
    ends = jnp.cumsum(lengths)
    starts = ends - lengths
    segment = jnp.sum((position[:, None] >= ends[None, :]).astype(jnp.int32), axis=1)
    belongs = segment[:, None] == jnp.arange(MAX_IMAGES, dtype=jnp.int32)[None, :]
    begin_at = jnp.sum(jnp.where(belongs, starts[None, :], 0), axis=1)
    size = jnp.sum(jnp.where(belongs, lengths[None, :], 0), axis=1)
    side = jnp.where(
        size == SIDE_S * SIDE_S, SIDE_S, jnp.where(size == SIDE_M * SIDE_M, SIDE_M, SIDE_L)
    ).astype(jnp.int32)
    offset = position - begin_at
    inside = segment < MAX_IMAGES
    row_at = jnp.where(inside, offset // side, 0)
    column_at = jnp.where(inside, offset % side, 0)
    return segment, row_at, column_at


def norm_parts(values):
    average = jnp.mean(values, axis=-1, keepdims=True)
    centred = values - average
    variance = jnp.mean(centred * centred, axis=-1, keepdims=True)
    inverse = lax.rsqrt(variance + EPS)
    return centred * inverse, inverse


def norm_grads(values, gain, incoming):
    xhat, inverse = norm_parts(values)
    grad_gain = jnp.sum(incoming * xhat, axis=0)
    grad_shift = jnp.sum(incoming, axis=0)
    scaled = incoming * gain
    through = inverse * (
        scaled
        - jnp.mean(scaled, axis=-1, keepdims=True)
        - xhat * jnp.mean(scaled * xhat, axis=-1, keepdims=True)
    )
    return through, grad_gain, grad_shift


def mm(left, right):
    return lax.dot_general(left, right, (((1,), (0,)), ((), ())), preferred_element_type=F32)


def mm_nt(left, right):
    return lax.dot_general(left, right, (((1,), (1,)), ((), ())), preferred_element_type=F32)


def mm_tn(left, right):
    return lax.dot_general(left, right, (((0,), (0,)), ((), ())), preferred_element_type=F32)


def turn(values, cosine, sine):
    half = HEAD_DIM // 2
    first, second = values[..., :half], values[..., half:]
    return jnp.concatenate(
        [first * cosine - second * sine, first * sine + second * cosine], axis=-1
    )


def masked_scores(query, key, allowed):
    scores = jnp.einsum("qhe,khe->hqk", query, key, preferred_element_type=F32) * (HEAD_DIM**-0.5)
    return jnp.where(allowed[None], scores, NEGATIVE)


def attend(query, key, value, allowed):
    scores = masked_scores(query, key, allowed)
    highest = jnp.max(scores, axis=-1, keepdims=True)
    exp_scores = jnp.exp(scores - highest)
    totals = jnp.sum(exp_scores, axis=-1, keepdims=True)
    probs = (exp_scores / totals).astype(BF)
    mixed = jnp.einsum("hqk,khe->qhe", probs, value, preferred_element_type=F32).astype(BF)
    return mixed, highest + jnp.log(totals)


def attend_back(query, key, value, allowed, log_totals, grad_mixed):
    scaling = HEAD_DIM**-0.5
    scores = masked_scores(query, key, allowed)
    probs = jnp.exp(scores - log_totals)
    low = probs.astype(BF)
    grad_value = jnp.einsum("hqk,qhe->khe", low, grad_mixed, preferred_element_type=F32)
    grad_probs = jnp.einsum("qhe,khe->hqk", grad_mixed, value, preferred_element_type=F32)
    grad_scores = (
        probs * (grad_probs - jnp.sum(probs * grad_probs, axis=-1, keepdims=True))
    ).astype(BF)
    grad_query = jnp.einsum("hqk,khe->qhe", grad_scores, key, preferred_element_type=F32) * scaling
    grad_key = jnp.einsum("hqk,qhe->khe", grad_scores, query, preferred_element_type=F32) * scaling
    return grad_query, grad_key, grad_value


def reduce_weight(parts):
    second = (parts[2] + over_core(parts[3].astype(BF)).astype(F32)).astype(BF)
    total = (
        parts[0] + over_core(parts[1].astype(BF)).astype(F32) + over_y(second).astype(F32)
    )
    me = lax.axis_index("dp")
    bits = lax.axis_size("dp").bit_length() - 1
    for bit in range(bits):
        half = total.shape[0] // 2
        mine = (me >> bit) & 1
        keep = lax.dynamic_slice_in_dim(total, mine * half, half, 0)
        send = lax.dynamic_slice_in_dim(total, (1 - mine) * half, half, 0)
        total = keep + over_bit(send.astype(BF), bit).astype(F32)
    total = total.astype(BF)
    for bit in reversed(range(bits)):
        other = over_bit(total, bit)
        mine = ((me >> bit) & 1) == 0
        total = jnp.concatenate(
            [jnp.where(mine, total, other), jnp.where(mine, other, total)], axis=0
        )
    return total.astype(F32)


def reduce_small(shared, split):
    rows = shared.shape[0]
    body = jnp.concatenate([shared] + list(split), axis=0)
    width = split[0].shape[0]
    other = over_core(body)
    mine = [split[at] + other[rows + (at ^ 1) * width : rows + ((at ^ 1) + 1) * width] for at in (0, 2)]
    both = shared + other[:rows]
    body = jnp.concatenate([both] + mine, axis=0)
    other = over_y(body)
    total = jnp.concatenate([both + other[:rows], mine[0] + other[rows + width :]], axis=0)
    for bit in range(lax.axis_size("dp").bit_length() - 1):
        total = total + over_bit(total, bit)
    return total[:rows], total[rows:]


def body(
    tokens,
    out_grad,
    image_lengths,
    norm1_gain,
    norm1_bias,
    qkv_weight,
    qkv_bias,
    rope_freqs,
    out_weight,
    out_bias,
    norm2_gain,
    norm2_bias,
    up_weight,
    up_bias,
    down_weight,
    down_bias,
):
    count, width = tokens.shape
    inner = qkv_weight.shape[3]
    heads = inner // HEAD_DIM
    hidden = up_weight.shape[2]
    me = lax.axis_index("tensor")
    lengths = lax.dynamic_index_in_dim(image_lengths, me // 2, 0, keepdims=False)
    half_at = me % 2
    position = jnp.arange(count, dtype=jnp.int32)
    segment, row_at, column_at = places_at(lengths, position + half_at * count)
    segment_other, _, _ = places_at(lengths, position + (1 - half_at) * count)
    allowed = segment[:, None] == jnp.concatenate([segment, segment_other])[None, :]
    row_at = row_at.astype(F32)
    column_at = column_at.astype(F32)

    small = jnp.concatenate(
        [qkv_bias.reshape(LAYERS, -1), rope_freqs.reshape(LAYERS, -1), up_bias], axis=1
    )
    small = quarters(small)
    weights = []
    for l in range(LAYERS):
        weights.append(
            (
                quarters(qkv_weight[l].reshape(-1, inner)),
                quarters(out_weight[l]),
                quarters(up_weight[l]),
                quarters(down_weight[l]),
            )
        )

    current = tokens.astype(F32)
    kept = []
    for l in range(LAYERS):
        qkv, out, up, down = weights[l]
        inputs = current
        xhat, _ = norm_parts(inputs)
        normed = (xhat * norm1_gain[l] + norm1_bias[l]).astype(BF)
        turned_q, turned_k, values, trig = [], [], [], []
        keys_all, values_all = [None] * 4, [None] * 4
        for j in range(4):
            bias = small[j][l, : 3 * inner].reshape(3, inner)
            freqs = small[j][l, 3 * inner : 3 * inner + 2 * inner // 2].reshape(2, heads, -1)
            angles = row_at[:, None, None] * freqs[0] + column_at[:, None, None] * freqs[1]
            cosine, sine = jnp.cos(angles), jnp.sin(angles)
            trig.append((cosine, sine))
            stack = qkv[j].reshape(3, width, inner)
            query, key, value = [(mm(normed, stack[i]) + bias[i]) for i in range(3)]
            turned_q.append(turn(query.reshape(count, heads, -1), cosine, sine).astype(BF))
            turned_k.append(turn(key.reshape(count, heads, -1), cosine, sine).astype(BF))
            values.append(value.astype(BF).reshape(count, heads, -1))
            if j % 2:
                sent = jnp.stack([turned_k[j - 1], values[j - 1], turned_k[j], values[j]])
                came = over_core(sent)
                for at, where in ((j - 1, 2), (j, 0)):
                    keys_all[at] = jnp.concatenate([turned_k[at], came[where]], axis=0)
                    values_all[at] = jnp.concatenate([values[at], came[where + 1]], axis=0)
        mixed, log_totals = [], []
        total = inputs + out_bias[l]
        for j in range(4):
            mixed_j, log_j = attend(turned_q[j], keys_all[j], values_all[j], allowed)
            mixed.append(mixed_j.reshape(count, inner))
            log_totals.append(log_j)
            total = total + mm(mixed[j], out[j])
        middle = total
        xhat, _ = norm_parts(middle)
        normed_mlp = (xhat * norm2_gain[l] + norm2_bias[l]).astype(BF)
        active, slope = [], []
        total = middle + down_bias[l]
        for j in range(4):
            pre = mm(normed_mlp, up[j]) + small[j][l, 4 * inner :]
            normal = 0.5 * (1.0 + lax.erf(pre * (0.5**0.5)))
            active.append((pre * normal).astype(BF))
            slope.append((normal + pre * jnp.exp(-0.5 * pre * pre) * 0.3989422804014327).astype(BF))
            total = total + mm(active[j], down[j])
        current = total
        kept.append(
            (inputs, normed, turned_q, keys_all, values_all, trig, mixed, log_totals, middle, normed_mlp, active, slope)
        )
    activations = current.astype(BF)

    gradient = out_grad.astype(F32)
    big = [None] * LAYERS
    shared_rows, split_rows = [], [[], [], [], []]
    for l in reversed(range(LAYERS)):
        qkv, out, up, down = weights[l]
        (inputs, normed, turned_q, keys_all, values_all, trig, mixed, log_totals, middle, normed_mlp, active, slope) = kept[l]
        low = gradient.astype(BF)
        grad_down_bias = jnp.sum(low.astype(F32), axis=0)
        grad_down, grad_up, grad_up_bias = [None] * 4, [None] * 4, [None] * 4
        total = None
        for j in (3, 2, 1, 0):
            grad_pre = (mm_nt(low, down[j]) * slope[j].astype(F32)).astype(BF)
            grad_down[j] = mm_tn(active[j], low)
            grad_up[j] = mm_tn(normed_mlp, grad_pre)
            grad_up_bias[j] = jnp.sum(grad_pre.astype(F32), axis=0)
            term = mm_nt(grad_pre, up[j])
            total = term if total is None else total + term
        grad_down = reduce_weight(grad_down)
        grad_up = reduce_weight(grad_up)
        through, grad_gain2, grad_shift2 = norm_grads(middle, norm2_gain[l], total)
        grad_middle = gradient + through
        low = grad_middle.astype(BF)
        grad_out_bias = jnp.sum(low.astype(F32), axis=0)
        grad_out, grad_qkv = [None] * 4, [None] * 4
        grad_qkv_bias, grad_freqs = [None] * 4, [None] * 4
        parts = [None] * 4
        total = None
        for pair in ((3, 2), (1, 0)):
            sent = []
            for j in pair:
                grad_out[j] = mm_tn(mixed[j], low)
                grad_mixed = mm_nt(low, out[j]).astype(BF).reshape(count, heads, -1)
                grad_q, grad_k, grad_v = attend_back(
                    turned_q[j], keys_all[j], values_all[j], allowed, log_totals[j], grad_mixed
                )
                parts[j] = (grad_q, grad_k[:count], grad_v[:count])
                sent += [grad_k[count:].astype(BF), grad_v[count:].astype(BF)]
            came = over_core(jnp.stack(sent))
            for at, j in enumerate(pair):
                grad_q, grad_k, grad_v = parts[j]
                grad_k = grad_k + came[2 * (1 - at)].astype(F32)
                grad_v = grad_v + came[2 * (1 - at) + 1].astype(F32)
                cosine, sine = trig[j]
                half = HEAD_DIM // 2
                angle = 0.0
                turned_back = []
                for grad, turned in ((grad_q, turned_q[j]), (grad_k, keys_all[j][:count])):
                    turned_back.append(turn(grad, cosine, -sine))
                    angle = angle + (
                        grad[..., half:] * turned[..., :half].astype(F32)
                        - grad[..., :half] * turned[..., half:].astype(F32)
                    )
                grad_freqs[j] = jnp.concatenate(
                    [
                        jnp.sum(row_at[:, None, None] * angle, axis=0).reshape(-1),
                        jnp.sum(column_at[:, None, None] * angle, axis=0).reshape(-1),
                    ]
                )
                grads = [
                    item.astype(BF).reshape(count, inner)
                    for item in (turned_back[0], turned_back[1], grad_v)
                ]
                stack = qkv[j].reshape(3, width, inner)
                grad_qkv[j] = jnp.concatenate([mm_tn(normed, item) for item in grads], axis=0)
                grad_qkv_bias[j] = jnp.concatenate([jnp.sum(item.astype(F32), axis=0) for item in grads])
                for i in range(3):
                    term = mm_nt(grads[i], stack[i])
                    total = term if total is None else total + term
        grad_out = reduce_weight(grad_out)
        grad_qkv = reduce_weight(grad_qkv)
        through, grad_gain1, grad_shift1 = norm_grads(inputs, norm1_gain[l], total)
        gradient = grad_middle + through
        big[l] = (grad_qkv.reshape(3, width, inner), grad_out, grad_up, grad_down)
        shared_rows = [grad_gain1, grad_shift1, grad_out_bias, grad_gain2, grad_shift2, grad_down_bias] + shared_rows
        for j in range(4):
            split_rows[j] = [jnp.concatenate([grad_qkv_bias[j], grad_freqs[j], grad_up_bias[j]]).reshape(-1, width)] + split_rows[j]

    shared, split = reduce_small(
        jnp.stack(shared_rows), [jnp.concatenate(rows, axis=0) for rows in split_rows]
    )
    shared = shared.reshape(LAYERS, 6, width)
    split = split.reshape(LAYERS, -1)
    stacked = [jnp.stack([big[l][item] for l in range(LAYERS)]) for item in range(4)]
    return (
        activations,
        gradient,
        shared[:, 0],
        shared[:, 1],
        stacked[0],
        split[:, : 3 * inner].reshape(LAYERS, 3, inner),
        split[:, 3 * inner : 4 * inner].reshape(LAYERS, 2, inner // 2),
        stacked[1],
        shared[:, 2],
        shared[:, 3],
        shared[:, 4],
        stacked[2],
        split[:, 4 * inner :],
        stacked[3],
        shared[:, 5],
    )


def solution(mesh):
    in_specs = (
        P(("dp", "tensor"), None),
        P(("dp", "tensor"), None),
        P("dp", None),
        P(),
        P(),
        P(None, None, None, "tensor"),
        P(None, None, "tensor"),
        P(None, None, "tensor"),
        P(None, "tensor", None),
        P(),
        P(),
        P(),
        P(None, None, "tensor"),
        P(None, "tensor"),
        P(None, "tensor", None),
        P(),
    )
    out_specs = (
        P(("dp", "tensor"), None),
        P(("dp", "tensor"), None),
        P(),
        P(),
        P(None, None, None, "tensor"),
        P(None, None, "tensor"),
        P(None, None, "tensor"),
        P(None, "tensor", None),
        P(),
        P(),
        P(),
        P(None, None, "tensor"),
        P(None, "tensor"),
        P(None, "tensor", None),
        P(),
    )
    return jax.shard_map(body, mesh=mesh, in_specs=in_specs, out_specs=out_specs, check_vma=False)
```

```python
from functools import partial

import jax
import jax.numpy as jnp
from jax import lax
from jax.experimental import pallas as pl
from jax.experimental.pallas import tpu as pltpu
from jax.sharding import PartitionSpec as P

HEAD_DIM = 64
LEN = 832
SIDE_S = 14
SIDE_M = 20
SIDE_L = 24
MAX_IMAGES = 4
LAYERS = 2

EPS = 1e-06
NEGATIVE = -1000000000.0
BF = jnp.bfloat16
F32 = jnp.float32

CORE = [(0, 1), (1, 0), (2, 3), (3, 2)]
ACROSS = [(0, 2), (2, 0), (1, 3), (3, 1)]


def over_core(values):
    return lax.ppermute(values, "tensor", CORE)


def over_y(values):
    return lax.ppermute(values, "tensor", ACROSS)


def over_bit(values, bit):
    size = lax.axis_size("dp")
    return lax.ppermute(values, "dp", [(at, at ^ (1 << bit)) for at in range(size)])


def places_at(lengths, position):
    ends = jnp.cumsum(lengths)
    starts = ends - lengths
    segment = jnp.sum((position[:, None] >= ends[None, :]).astype(jnp.int32), axis=1)
    belongs = segment[:, None] == jnp.arange(MAX_IMAGES, dtype=jnp.int32)[None, :]
    begin_at = jnp.sum(jnp.where(belongs, starts[None, :], 0), axis=1)
    size = jnp.sum(jnp.where(belongs, lengths[None, :], 0), axis=1)
    side = jnp.where(
        size == SIDE_S * SIDE_S, SIDE_S, jnp.where(size == SIDE_M * SIDE_M, SIDE_M, SIDE_L)
    ).astype(jnp.int32)
    offset = position - begin_at
    inside = segment < MAX_IMAGES
    row_at = jnp.where(inside, offset // side, 0)
    column_at = jnp.where(inside, offset % side, 0)
    return segment, row_at, column_at


PLANS = (
    (((3, 2), (5, 1), (6, 1), (7, 1), (8, 1), (9, 1), (10, 1)), ((4, 1), (5, 1), (6, 1), (7, 1), (8, 1), (9, 1), (10, 1))),
    (
        ((3, 2), (5, 1), (6, 1), (7, 1), (8, 1), (9, 1), (10, 1)),
        ((5, 1), (6, 1), (7, 1), (8, 1), (9, 1), (10, 1), (11, 1)),
    ),
)
SMALL_PLAN = ((1, 1), (2, 1), (3, 1), (4, 1), (5, 1), (6, 1))
VMEM_BYTES = 58 * 2**20
PARAMS = pltpu.CompilerParams(vmem_limit_bytes=VMEM_BYTES)
WHOLE = pl.BlockSpec(memory_space=pltpu.VMEM)
PLACE = pl.BlockSpec(memory_space=pl.ANY)
SCALAR = pl.BlockSpec(memory_space=pltpu.SMEM)
HALF = HEAD_DIM // 2
SIDE_ROWS = 32
SMALL_ROWS = 16


def dot(left, right, on_left, on_right):
    return lax.dot_general(
        left, right, (((on_left,), (on_right,)), ((), ())), preferred_element_type=F32
    )


def norm_parts(values):
    average = jnp.mean(values, axis=-1, keepdims=True)
    centred = values - average
    variance = jnp.mean(centred * centred, axis=-1, keepdims=True)
    inverse = lax.rsqrt(variance + EPS)
    return centred * inverse, inverse


def norm_back(values, gain, incoming):
    xhat, inverse = norm_parts(values)
    grad_gain = jnp.sum(incoming * xhat, axis=0, keepdims=True)
    grad_shift = jnp.sum(incoming, axis=0, keepdims=True)
    scaled = incoming * gain
    through = inverse * (
        scaled
        - jnp.mean(scaled, axis=-1, keepdims=True)
        - xhat * jnp.mean(scaled * xhat, axis=-1, keepdims=True)
    )
    return through, grad_gain, grad_shift


def first_half(shape):
    return lax.broadcasted_iota(jnp.int32, shape, 1) % HEAD_DIM < HALF


def swap(values):
    width = values.shape[1]
    return jnp.where(
        first_half(values.shape),
        pltpu.roll(values, width - HALF, 1),
        pltpu.roll(values, HALF, 1),
    )


def one_head(values, head):
    lane = lax.broadcasted_iota(jnp.int32, values.shape, 1)
    return jnp.where((lane < HEAD_DIM) == (head == 0), values, jnp.zeros_like(values))


def join_heads(first, second):
    lane = lax.broadcasted_iota(jnp.int32, first.shape, 1)
    return jnp.where(lane < HEAD_DIM, first, second)


class Held:
    def __init__(self, source, buffer, sem):
        self.copy, self.buffer, self.done = pltpu.make_async_copy(source, buffer, sem), buffer, False
        self.shape, self.dtype = buffer.shape, buffer.dtype
        self.copy.start()

    def wait(self):
        if not self.done:
            self.copy.wait()
            self.done = True

    def __getitem__(self, at):
        self.wait()
        return self.buffer[at]


class Given:
    def __init__(self, target, buffer, sems):
        self.target, self.buffer, self.sems, self.copies = target, buffer, sems, []

    def __setitem__(self, at, values):
        self.buffer[at] = values

    def __getitem__(self, at):
        return self.buffer[at]

    def leave(self, at=None):
        source, target = self.buffer, self.target
        if at is not None:
            source, target = source.at[at], target.at[at]
        self.copies.append(pltpu.make_async_copy(source, target, self.sems.at[len(self.copies)]))
        self.copies[-1].start()


PIECES_OUT = 6


def staged(body, name, flops, scalars, inputs, raws, outs, raw_outs=(), scratch=(), gates=()):
    counts = [len(inputs), len(raws), len(gates), len(outs), len(raw_outs)]

    def kernel(numbers, *refs):
        groups = []
        for count in counts:
            groups.append(refs[:count])
            refs = refs[count:]
        sources, plain, _, targets, plain_targets = groups
        in_buffers, out_buffers, rest = refs[: counts[0]], refs[counts[0] : counts[0] + counts[3]], refs[counts[0] + counts[3] :]
        in_sems, out_sems, rest = rest[0], rest[1], rest[2:]
        held = [Held(*item, in_sems.at[at]) for at, item in enumerate(zip(sources, in_buffers))]
        given = [Given(*item, out_sems.at[at]) for at, item in enumerate(zip(targets, out_buffers))]
        body(numbers, held, plain, given, plain_targets, *rest)
        for item in held:
            item.wait()
        for item in given:
            if not item.copies:
                item.leave()
        for item in given:
            for copy in item.copies:
                copy.wait()

    return pl.pallas_call(
        kernel,
        out_shape=list(outs) + list(raw_outs),
        in_specs=[SCALAR] + [PLACE] * sum(counts[:3]),
        out_specs=[PLACE] * sum(counts[3:]),
        scratch_shapes=[pltpu.VMEM(item.shape, item.dtype) for item in list(inputs) + list(outs)]
        + [pltpu.SemaphoreType.DMA((max(counts[0], 1),)), pltpu.SemaphoreType.DMA((max(counts[3], 1), PIECES_OUT))]
        + list(scratch),
        compiler_params=PARAMS,
        name=name,
        cost_estimate=pl.CostEstimate(flops=flops // 8, bytes_accessed=2**20, transcendentals=0),
    )(scalars, *inputs, *raws, *gates)


def fetch(pairs, sems):
    copies = [pltpu.make_async_copy(source, target, sems.at[at]) for at, (source, target) in enumerate(pairs)]
    for copy in copies:
        copy.start()
    return copies


def att_pairs(near, refs, into, xbit, parts):
    inner = into.shape[1] // 2
    low, high = pl.ds(0, inner), pl.ds(inner, inner)
    if near:
        return [(refs[0].at[pl.ds(0, parts)], into.at[pl.ds(0, parts), low]), (refs[1].at[pl.ds(0, parts)], into.at[pl.ds(0, parts), high])]
    mine, other = pl.ds(2 * xbit, 2), pl.ds(2 - 2 * xbit, 2)
    return [
        (refs[0], into.at[mine, low]),
        (refs[1], into.at[other, low]),
        (refs[2], into.at[mine, high]),
        (refs[3], into.at[other, high]),
    ]


def mlp_pairs(near, refs, into, xbit):
    if near:
        return [(ref, into.at[quarter]) for quarter, ref in enumerate(refs)]
    slots = ((0, xbit), (0, 1 - xbit), (1, xbit), (1, 1 - xbit))
    return [(ref, into.at[quarter, slot]) for ref, (quarter, slot) in zip(refs, slots)]


def pack(layer, x_bit, first, second, cut, gates=()):
    _, rows, width, inner = first.shape
    more = second.shape[1]

    def body(numbers, _, raws, __, targets, held, sems):
        whole, half = targets
        for copy in fetch(
            [(raws[0].at[layer], held.at[pl.ds(0, rows)]), (raws[1].at[layer], held.at[pl.ds(rows, more)])], sems
        ):
            copy.wait()
        copies = [
            pltpu.make_async_copy(held.at[pl.ds(cut * numbers[0], cut)], half, sems.at[2]),
            pltpu.make_async_copy(held, whole, sems.at[3]),
        ]
        for copy in copies:
            copy.start()
        for copy in copies:
            copy.wait()

    return staged(
        body, "pack", 0, x_bit, (), (first, second), (),
        (
            jax.ShapeDtypeStruct((rows + more, width, inner), BF),
            jax.ShapeDtypeStruct((cut, width, inner), BF),
        ),
        (pltpu.VMEM((rows + more, width, inner), BF), pltpu.SemaphoreType.DMA((4,))), gates,
    )


def angle_tables(freqs, places):
    steps = lax.broadcasted_iota(jnp.int32, (SIDE_ROWS, 1), 0).astype(F32)
    found = []
    for axis in range(2):
        terms = steps * freqs[axis]
        table = jnp.concatenate([jnp.cos(terms), jnp.sin(terms)], axis=1)
        at = places[:, axis : axis + 1]
        column = lax.broadcasted_iota(jnp.int32, (places.shape[0], SIDE_ROWS), 1).astype(F32)
        chosen = lax.dot_general(
            (column == at).astype(F32), table, (((1,), (0,)), ((), ())),
            precision=lax.Precision.HIGHEST, preferred_element_type=F32,
        )
        width = terms.shape[1]
        found.append((chosen[:, :width], chosen[:, width:]))
    (row_cos, row_sin), (col_cos, col_sin) = found
    cosine = row_cos * col_cos - row_sin * col_sin
    sine = row_sin * col_cos + row_cos * col_sin
    return cosine, jnp.where(first_half(sine.shape), -sine, sine)


def qkv_part(near, layer, x_bit, source, gain, shift, small, places, weights, gates=()):
    count, width = source.shape
    inner = weights[0].shape[1]

    def body(numbers, inputs, raws, results, _, held, sems):
        gain, shift, places, first, second, source = inputs
        query, kept, sent, cosine, sine = results[:5]
        copies = fetch(att_pairs(near, raws, held, numbers[0], 3), sems)
        both = [item[layer : layer + 1] for item in (first, second)]
        bias = [
            jnp.concatenate([item[:, part * inner : (part + 1) * inner] for item in both], axis=1)
            for part in range(3)
        ]
        freqs = []
        for axis in range(2):
            begin = 3 * inner + axis * (inner // 2)
            pieces = [item[:, at : at + HALF] for item in both for at in range(begin, begin + inner // 2, HALF)]
            freqs.append(jnp.concatenate([piece for piece in pieces for _ in range(2)], axis=1))
        cosine[...], sine[...] = angle_tables(freqs, places[...])
        cosine.leave()
        sine.leave()
        if near:
            xhat, _ = norm_parts(source[...].astype(F32))
            normed = (xhat * gain[...] + shift[...]).astype(BF)
            results[5][...] = normed
            results[5].leave()
        else:
            normed = source[...]
        for copy in copies:
            copy.wait()
        for part in (1, 2, 0):
            values = dot(normed, held[part], 1, 1) + bias[part]
            if part < 2:
                values = values * cosine[...] + swap(values) * sine[...]
            if part == 0:
                query[...] = (values * HEAD_DIM**-0.5).astype(BF)
            else:
                kept[part - 1] = values.astype(BF)
                sent[part - 1] = pltpu.roll(values, inner, 1).astype(BF)
                sent.leave(part - 1)

    pair = jax.ShapeDtypeStruct((2, count, 2 * inner), BF)
    table = jax.ShapeDtypeStruct((count, 2 * inner), F32)
    outs = [jax.ShapeDtypeStruct((count, 2 * inner), BF), pair, pair, table, table]
    if near:
        outs.append(jax.ShapeDtypeStruct((count, width), BF))
    return staged(
        body, "qkv_near" if near else "qkv_far", 2 * count * width * 6 * inner, x_bit,
        (gain, shift, places, *small, source), weights, outs,
        scratch=(pltpu.VMEM((4, 2 * inner, width), BF), pltpu.SemaphoreType.DMA((len(weights),))), gates=gates,
    )


def attend(query, kept, came, here, there, number, gates=()):
    count, width = query.shape
    heads = width // HEAD_DIM

    def body(_, inputs, __, results, ___):
        query, kept, here, came, there = inputs
        mixed, spread, exps = results
        allowed = here[...] == there[...]
        for pair in range(heads // 2):
            lanes = slice(2 * HEAD_DIM * pair, 2 * HEAD_DIM * (pair + 1))
            keys = jnp.concatenate([kept[0, :, lanes], came[0, :, lanes]], axis=0)
            values = jnp.concatenate([kept[1, :, lanes], came[1, :, lanes]], axis=0)
            outs, inverses = [], []
            for head in range(2):
                scores = dot(one_head(query[:, lanes], head), keys, 1, 1)
                scores = jnp.where(allowed, scores, NEGATIVE)
                highest = jnp.max(scores, axis=1, keepdims=True)
                raised = jnp.exp(scores - highest)
                inverse = 1.0 / jnp.sum(raised, axis=1, keepdims=True)
                low = raised.astype(BF)
                exps[2 * pair + head] = low
                exps.leave(2 * pair + head)
                outs.append(dot(low, values, 1, 0) * inverse)
                inverses.append(jnp.broadcast_to(inverse, outs[0].shape))
            mixed[:, lanes] = join_heads(*outs).astype(BF)
            spread[:, lanes] = join_heads(*inverses)

    return staged(
        body, "attend", 8 * count * width * 768, number, (query, kept, here, came, there), (),
        (
            jax.ShapeDtypeStruct((count, width), BF),
            jax.ShapeDtypeStruct((count, width), F32),
            jax.ShapeDtypeStruct((heads, count, 2 * count), BF),
        ),
        gates=gates,
    )


def gelu_parts(pre):
    size = jnp.abs(pre)
    ratio = 1.0 / (1.0 + 0.3275911 * (0.5**0.5) * size)
    bell = jnp.exp(-0.5 * pre * pre)
    poly = ((((0.5 * 1.061405429 * ratio - 0.5 * 1.453152027) * ratio + 0.5 * 1.421413741) * ratio - 0.5 * 0.284496736) * ratio + 0.5 * 0.254829592) * ratio
    below = poly * bell
    normal = jnp.where(pre < 0, below, 1.0 - below)
    return pre * normal, normal + pre * (bell * 0.3989422804014327)


def feed(quarter, normed, held, up_bias, active, slope):
    value, rate = gelu_parts(dot(normed, held[quarter, 0], 1, 0) + up_bias[quarter])
    low = value.astype(BF)
    active[quarter] = low
    active.leave(quarter)
    slope[quarter] = rate.astype(BF)
    slope.leave(quarter)
    return dot(low, held[quarter, 1], 1, 0)


def mlp_near(layer, x_bit, inputs, mixed_near, mixed_far, out_bias, gain, shift, small, down_bias, outs, weights, gates=()):
    count, width = inputs.shape
    hidden = weights[0].shape[2]
    inner = outs[0].shape[1]

    def body(numbers, held_inputs, raws, results, _, held_out, held, sems):
        mixed_near, mixed_far, inputs, out_bias, gain, shift, first, second, down_bias = held_inputs
        up_bias = [item[layer : layer + 1, width:] for item in (first, second)]
        middle, normed_out, active, slope, total = results
        xbit = numbers[0]
        copies = fetch(
            [
                (raws[0].at[3], held_out.at[0]),
                (raws[1].at[3], held_out.at[1]),
                (raws[2].at[1], held_out.at[2 + 2 * (1 - xbit)]),
                (raws[3].at[1], held_out.at[2 + 2 * xbit]),
                (raws[4].at[1], held_out.at[3 + 2 * (1 - xbit)]),
                (raws[5].at[1], held_out.at[3 + 2 * xbit]),
            ]
            + mlp_pairs(True, raws[6:], held, xbit),
            sems,
        )
        for copy in copies[:6]:
            copy.wait()
        centre = dot(mixed_near[...], jnp.concatenate([held_out[0], held_out[1]], axis=0), 1, 0)
        centre = centre + dot(mixed_far[...], jnp.concatenate([held_out[2], held_out[3]], axis=0), 1, 0)
        centre = centre + inputs[...].astype(F32) + out_bias[...]
        middle[...] = centre
        middle.leave()
        xhat, _ = norm_parts(centre)
        normed = (xhat * gain[...] + shift[...]).astype(BF)
        normed_out[...] = normed
        normed_out.leave()
        gathered = centre + down_bias[...]
        for quarter in range(2):
            copies[6 + quarter].wait()
            gathered = gathered + feed(quarter, normed, held, up_bias, active, slope)
        total[...] = gathered

    kept = jax.ShapeDtypeStruct((2, count, hidden), BF)
    full = jax.ShapeDtypeStruct((count, width), F32)
    return staged(
        body, "mlp_near", 10 * count * width * width, x_bit,
        (mixed_near, mixed_far, inputs, out_bias, gain, shift, *small, down_bias), tuple(outs) + tuple(weights),
        (full, jax.ShapeDtypeStruct((count, width), BF), kept, kept, full),
        scratch=(
            pltpu.VMEM((6, inner, width), BF),
            pltpu.VMEM((2, 2, width, hidden), BF),
            pltpu.SemaphoreType.DMA((8,)),
        ),
        gates=gates,
    )


def mlp_far(layer, x_bit, normed, total, small, weights, dtype, gates=()):
    count, width = normed.shape
    hidden = weights[0].shape[1]

    def body(numbers, inputs, raws, results, _, held, sems):
        normed, first, second, total = inputs
        up_bias = [item[layer : layer + 1, width:] for item in (first, second)]
        active, slope, result = results
        copies = fetch(mlp_pairs(False, raws, held, numbers[0]), sems)
        gathered = None
        for quarter in range(2):
            for copy in copies[2 * quarter : 2 * quarter + 2]:
                copy.wait()
            term = feed(quarter, normed[...], held, up_bias, active, slope)
            gathered = total[...] + term if gathered is None else gathered + term
        result[...] = gathered.astype(dtype)

    kept = jax.ShapeDtypeStruct((2, count, hidden), BF)
    return staged(
        body, "mlp_far", 8 * count * width * width, x_bit, (normed, *small, total), weights,
        (kept, kept, jax.ShapeDtypeStruct((count, width), dtype)),
        scratch=(pltpu.VMEM((2, 2, width, hidden), BF), pltpu.SemaphoreType.DMA((4,))), gates=gates,
    )


def mlp_back(x_bit, gradient, normed, middle, gain, active, slope, near, far, gates=()):
    count, width = normed.shape
    hidden = active[0].shape[2]

    def body(numbers, inputs, raws, results, grads, held, ready, sems, out_sems):
        gradient, active_far, slope_far, normed, active_near, slope_near, gain, middle = inputs
        bias_grad, sums, grad_middle, low_middle = results
        xbit, up_slot = numbers[0], numbers[1]
        targets = (grads[0:1], grads[1:5], grads[5:6], grads[6:10])
        copies = fetch(
            mlp_pairs(False, raws[2:], held.at[pl.ds(2, 2)], xbit) + mlp_pairs(True, raws[:2], held.at[pl.ds(0, 2)], xbit), sems
        )
        needed = ((copies[4],), (copies[5],), copies[0:2], copies[2:4])
        leaving = []

        def leave(quarter, kind, slot, values):
            ready[quarter, kind] = values.astype(BF)
            rows = targets[quarter][0].shape[1]
            for at, target in enumerate(targets[quarter]):
                copy = pltpu.make_async_copy(
                    ready.at[quarter, kind, pl.ds(at * rows, rows)], target.at[slot], out_sems.at[len(leaving)]
                )
                copy.start()
                leaving.append(copy)

        incoming = gradient[...].astype(F32)
        low = incoming.astype(BF)
        gathered = None
        for quarter in (3, 2, 1, 0):
            active, slope = (active_near, slope_near) if quarter < 2 else (active_far, slope_far)
            leave(quarter, 0, 1 - up_slot, dot(active[quarter % 2], low, 0, 0))
            for copy in needed[quarter]:
                copy.wait()
            inside = dot(low, held[quarter, 1], 1, 1) * slope[quarter % 2].astype(F32)
            low_inside = inside.astype(BF)
            bias_grad[quarter : quarter + 1] = jnp.sum(low_inside.astype(F32), axis=0, keepdims=True)
            leave(quarter, 1, up_slot, dot(normed[...], low_inside, 0, 0))
            term = dot(low_inside, held[quarter, 0], 1, 1)
            gathered = term if gathered is None else gathered + term
        through, grad_gain, grad_shift = norm_back(middle[...], gain[...], gathered)
        result = incoming + through
        grad_middle[...] = result
        grad_middle.leave()
        low_result = result.astype(BF)
        low_middle[...] = low_result
        low_middle.leave()
        sums[0:1] = grad_gain
        sums[1:2] = grad_shift
        sums[2:3] = jnp.sum(low_result.astype(F32), axis=0, keepdims=True)
        sums[3:4] = jnp.sum(low.astype(F32), axis=0, keepdims=True)
        for copy in leaving:
            copy.wait()

    whole = jax.ShapeDtypeStruct((2, width, hidden), BF)
    part = jax.ShapeDtypeStruct((2, width // 4, hidden), BF)
    outs = [
        jax.ShapeDtypeStruct((4, hidden), F32),
        jax.ShapeDtypeStruct((4, width), F32),
        jax.ShapeDtypeStruct((count, width), F32),
        jax.ShapeDtypeStruct((count, width), BF),
    ]
    found = staged(
        body, "mlp_back", 32 * count * width * width, x_bit,
        (gradient, active[1], slope[1], normed, active[0], slope[0], gain, middle), tuple(near) + tuple(far), outs,
        ([whole] + [part] * 4) * 2,
        (
            pltpu.VMEM((4, 2, width, hidden), BF),
            pltpu.VMEM((4, 2, width, hidden), BF),
            pltpu.SemaphoreType.DMA((6,)),
            pltpu.SemaphoreType.DMA((20,)),
        ),
        gates,
    )
    return (found[4], found[5:9], found[9], found[10:14]), found[:4]


def attend_back(x_bit, incoming, sides, near, far, gates=()):
    count, width = sides[0][0].shape
    pairs = width // (2 * HEAD_DIM)
    inner, full = near[0].shape[1:]

    def body(numbers, inputs, raws, results, _, held, sems):
        incoming, xbit = inputs[0], numbers[0]
        copies = fetch(
            [
                (raws[0].at[3], held.at[0]),
                (raws[1].at[3], held.at[1]),
                (raws[2].at[1], held.at[2 + 2 * (1 - xbit)]),
                (raws[3].at[1], held.at[2 + 2 * xbit]),
                (raws[4].at[1], held.at[3 + 2 * (1 - xbit)]),
                (raws[5].at[1], held.at[3 + 2 * xbit]),
            ],
            sems,
        )
        for copy in copies:
            copy.wait()
        for side in (0, 1):
            mixed, spread, kept, came, query, exps = inputs[1 + 6 * side : 7 + 6 * side]
            grad_query, grad_kept, *grad_sent = results[4 * side : 4 * side + 4]
            both = jnp.concatenate([held[2 * side], held[2 * side + 1]], axis=0)
            scaled = dot(incoming[...], both, 1, 1) * spread[...]
            product_all = scaled * mixed[...].astype(F32)
            low_all = scaled.astype(BF)
            for pair in range(pairs):
                lanes = slice(2 * HEAD_DIM * pair, 2 * HEAD_DIM * (pair + 1))
                keys = jnp.concatenate([kept[0, :, lanes], came[0, :, lanes]], axis=0)
                values = jnp.concatenate([kept[1, :, lanes], came[1, :, lanes]], axis=0)
                low_mixed, product = low_all[:, lanes], product_all[:, lanes]
                for_query, for_key, for_value = [], [], []
                for head in range(2):
                    raised = exps[2 * pair + head]
                    level = jnp.sum(one_head(product, head), axis=1, keepdims=True)
                    grad_probs = dot(one_head(low_mixed, head), values, 1, 1)
                    grad_scores = (raised.astype(F32) * (grad_probs - level)).astype(BF)
                    for_value.append(dot(raised, low_mixed, 0, 0))
                    for_query.append(dot(grad_scores, keys, 1, 0))
                    for_key.append(dot(grad_scores, query[:, lanes], 0, 0))
                grad_query[:, lanes] = join_heads(*for_query).astype(BF)
                for part, both_heads in enumerate((for_key, for_value)):
                    joined = join_heads(*both_heads).astype(BF)
                    grad_kept[part, :, lanes] = joined[:count]
                    grad_sent[part][:, lanes] = joined[count:]
            for item in results[4 * side : 4 * side + 4]:
                item.leave()

    shapes = [
        jax.ShapeDtypeStruct((count, width), BF),
        jax.ShapeDtypeStruct((2, count, width), BF),
        jax.ShapeDtypeStruct((count, width), BF),
        jax.ShapeDtypeStruct((count, width), BF),
    ]
    ordered = [incoming]
    for query, kept, came, mixed, spread, exps in sides:
        ordered += [mixed, spread, kept, came, query, exps]
    found = staged(
        body, "attend_back", 32 * count * width * full, x_bit, ordered, tuple(near) + tuple(far), shapes * 2,
        scratch=(pltpu.VMEM((6, inner, full), BF), pltpu.SemaphoreType.DMA((6,))),
        gates=gates,
    )
    return found[:4], found[4:]


def qkv_back(x_bit, normed, incoming, places, sides, near, far, gain, inputs_kept, grad_middle, little, gates=()):
    count, width = normed.shape
    inner = near[0].shape[1]

    def body(numbers, inputs, raws, results, grads, held, ready, sems, out_sems):
        normed, incoming, places = inputs[:3]
        gain, inputs_kept, grad_middle, sums2, up_bias_grad = inputs[21:26]
        rows_out, result = results
        earlier = inputs[26:]
        base = SMALL_ROWS * len(earlier)
        for at, item in enumerate(earlier):
            rows_out[SMALL_ROWS * at : SMALL_ROWS * (at + 1)] = item[...]
        xbit = numbers[0]
        targets = (grads[0:1], grads[1:5], grads[5:6], grads[6:10])
        copies = fetch(
            att_pairs(False, raws[2:], held.at[1], xbit, 3) + att_pairs(True, raws[:2], held.at[0], xbit, 3), sems
        )
        needed = (copies[4:], copies[:4])
        slots = (2 * xbit, 2 * xbit + 1, 2 - 2 * xbit, 3 - 2 * xbit)
        leaving = []

        def store(side, part, values):
            ready[side, part] = values.astype(BF)
            for quarter in range(2):
                rows = targets[2 * side + quarter][0].shape[1]
                for at, target in enumerate(targets[2 * side + quarter]):
                    copy = pltpu.make_async_copy(
                        ready.at[side, part, pl.ds(quarter * inner + at * rows, rows)],
                        target.at[slots[part]],
                        out_sems.at[len(leaving)],
                    )
                    copy.start()
                    leaving.append(copy)

        gathered = None
        for side in (1, 0):
            mixed, grad_query, query, grad_kept, came_key, came_value, kept, cosine, sine = inputs[3 + 9 * side : 12 + 9 * side]
            lanes = slice(2 * inner * side, 2 * inner * (side + 1))
            store(side, 3, dot(mixed[...], incoming[...], 0, 0))
            sign = jnp.where(first_half(query.shape), -1.0, 1.0)
            raw_query = grad_query[...].astype(F32)
            raw_key = grad_kept[0].astype(F32) + pltpu.roll(came_key[...].astype(F32), inner, 1)
            raw_value = grad_kept[1].astype(F32) + pltpu.roll(came_value[...].astype(F32), inner, 1)
            angle = (raw_query * swap(query[...].astype(F32)) + raw_key * swap(kept[0].astype(F32))) * sign
            for axis in range(2):
                rows_out[base + 13 + axis : base + 14 + axis, lanes] = jnp.sum(
                    angle * places[:, axis : axis + 1], axis=0, keepdims=True
                )
            cos, sin = cosine[...], sine[...]
            turned = (
                (raw_query * cos - swap(raw_query) * sin) * HEAD_DIM**-0.5,
                raw_key * cos - swap(raw_key) * sin,
                raw_value,
            )
            lows = [item.astype(BF) for item in turned]
            for part in range(3):
                rows_out[base + 10 + part : base + 11 + part, lanes] = jnp.sum(
                    lows[part].astype(F32), axis=0, keepdims=True
                )
                store(side, part, dot(lows[part], normed[...], 0, 0))
            for copy in needed[side]:
                copy.wait()
            for part in range(3):
                term = dot(lows[part], held[side, part], 1, 0)
                gathered = term if gathered is None else gathered + term
        through, grad_gain, grad_shift = norm_back(inputs_kept[...].astype(F32), gain[...], gathered)
        result[...] = grad_middle[...] + through
        rows_out[base : base + 1] = grad_gain
        rows_out[base + 1 : base + 2] = grad_shift
        rows_out[base + 2 : base + 3] = sums2[2:3]
        rows_out[base + 3 : base + 5] = sums2[0:2]
        rows_out[base + 5 : base + 6] = sums2[3:4]
        rows_out[base + 6 : base + 10] = up_bias_grad[...]
        rows_out[base + 15 : base + 16] = jnp.zeros((1, rows_out.buffer.shape[1]), F32)
        for copy in leaving:
            copy.wait()

    rows = SMALL_ROWS * (len(little) - 1)
    outs = [jax.ShapeDtypeStruct((rows, width), F32), jax.ShapeDtypeStruct((count, width), F32)]
    whole = jax.ShapeDtypeStruct((4, inner, width), BF)
    part = jax.ShapeDtypeStruct((4, inner // 4, width), BF)
    ordered = [normed, incoming, places]
    for grad_query, grad_kept, came_key, came_value, query, kept, cosine, sine, mixed in sides:
        ordered += [mixed, grad_query, query, grad_kept, came_key, came_value, kept, cosine, sine]
    found = staged(
        body, "qkv_back", 32 * count * width * 2 * inner, x_bit,
        ordered + [gain, inputs_kept, grad_middle] + list(little), tuple(near) + tuple(far), outs,
        ([whole] + [part] * 4) * 2,
        (
            pltpu.VMEM((2, 4, 2 * inner, width), BF),
            pltpu.VMEM((2, 4, 2 * inner, width), BF),
            pltpu.SemaphoreType.DMA((6,)),
            pltpu.SemaphoreType.DMA((40,)),
        ),
        gates,
    )
    return (found[2], found[3:7], found[7], found[8:12]), found[:2]


def run_tasks(place, tasks, gates):
    inputs = [item for task in tasks for item in task[0]]
    outs = [jax.ShapeDtypeStruct(*item) for task in tasks for item in task[1]]

    def body(at, sources, _, results, __):
        for task in tasks:
            task[2](at[0], sources[: len(task[0])], results[: len(task[1])])
            sources, results = sources[len(task[0]) :], results[len(task[1]) :]

    found = staged(body, "sums", 0, place, inputs, (), outs, gates=gates)
    given = []
    for task in tasks:
        given.append(found[: len(task[1])])
        found = found[len(task[1]) :]
    return given


def wide(ref):
    return ref[...].astype(F32)


class Piece:
    def begin(self, found):
        self.own, first, self.second, third = found
        self.came_near = [over_core(item) for item in first]
        self.came_far = [over_core(item) for item in third]
        return self.came_near + self.came_far

    def sources(self):
        return (self.own, self.second, *self.came_near, *self.came_far)

    def sum_of(self, sources, quarter, slot, high):
        mine = sources[quarter]
        parts = sources[2 + 4 * quarter : 6 + 4 * quarter]
        if mine.shape[0] == 2:
            rows = mine.shape[1] // 2
            own = mine[slot, high * rows : (high + 1) * rows]
            came = jnp.concatenate([parts[2 * high][slot], parts[2 * high + 1][slot]], axis=0)
        else:
            own = mine[2 * slot + high]
            came = jnp.concatenate([part[2 * slot + high] for part in parts], axis=0)
        return own.astype(F32) + came.astype(F32)

    def size(self):
        slots, rows, width = self.own.shape
        return slots * rows // 4, width

    def cross(self):
        half, width = self.size()

        def sums(at, sources, results):
            del at
            for slot in range(2):
                results[0][slot] = self.sum_of(sources, 1, slot, 0).astype(BF)
                results[1][slot] = self.sum_of(sources, 0, slot, 0).astype(BF)
                results[2 + slot][0] = self.sum_of(sources, 0, slot, 1).astype(BF)
                results[2 + slot][1] = self.sum_of(sources, 1, slot, 1).astype(BF)

        def after(found):
            up, self.low, self.high, away = found
            self.across, self.sideways = over_y(up), over_bit(away, 0)
            return [self.across, self.sideways]

        return self.sources(), [((2, half, width), BF)] * 4, sums, after

    def turn(self):
        _, half, width = self.low.shape

        def sums(at, sources, results):
            del at
            for way in range(2):
                results[2 * way][...] = sources[2 * way][0].astype(F32) + sources[2 * way + 1][0].astype(F32)
                results[2 * way + 1][...] = (
                    sources[2 * way][1].astype(F32) + sources[2 * way + 1][1].astype(F32)
                ).astype(BF)

        def after(found):
            self.low_kept, low, self.high_kept, high = found
            self.low_came, self.high_came = over_bit(low, 0), over_y(high)
            return [self.low_came, self.high_came]

        shapes = [((half, width), F32), ((half, width), BF)] * 2
        return (self.low, self.across, self.high, self.sideways), shapes, sums, after

    def total_parts(self):
        if self.kept is None:
            inputs = (self.low_kept, self.low_came, self.high_kept, self.high_came)
            rows, width = self.low_kept.shape

            def total(sources):
                low, high = wide(sources[0]) + wide(sources[1]), wide(sources[2]) + wide(sources[3])
                return jnp.concatenate([low, high], axis=0)

            return inputs, 2 * rows, width, total

        def total(sources):
            result = wide(sources[0])
            for source in sources[1:]:
                result = result + wide(source)
            return result

        return (self.kept,) + tuple(self.came), self.kept.shape[0], self.kept.shape[1], total

    def halve(self, bit):
        inputs, rows, width, total_of = self.total_parts()
        half = rows // 2

        def sums(at, sources, results):
            total = total_of(sources)
            low, high = total[:half], total[half:]
            first = ((at >> bit) & 1) == 0
            results[0][...] = jnp.where(first, low, high)
            results[1][...] = jnp.where(first, high, low).astype(BF)

        def after(found):
            self.kept = found[0]
            self.came = (over_bit(found[1], bit),)
            return list(self.came)

        return inputs, [((half, width), F32), ((half, width), BF)], sums, after

    def whole(self):
        inputs, rows, width, total_of = self.total_parts()

        def sums(at, sources, results):
            del at
            results[0][...] = total_of(sources).astype(BF)

        return inputs, [((rows, width), BF)], sums, self.spread

    def spread(self, found):
        self.total = found[0]
        self.others = (over_bit(self.total, self.ways.pop()),)
        return list(self.others)

    def join(self, bit):
        rows, width = self.total.shape

        def sums(at, sources, results):
            first = ((at >> bit) & 1) == 0
            mine, other = sources[0][...], sources[1][...]
            results[0][:rows] = jnp.where(first, mine, other)
            results[0][rows:] = jnp.where(first, other, mine)

        return (self.total,) + self.others, [((2 * rows, width), BF)], sums, self.spread

    def tasks(self):
        bits = lax.axis_size("dp").bit_length() - 1
        self.kept = None
        calls = [self.cross, self.turn] + [partial(self.halve, bit) for bit in range(1, bits)]
        calls += [self.whole] + [partial(self.join, bit) for bit in reversed(range(1, bits))]
        self.ways = list(range(bits))
        return calls

    def result(self, bit):
        return (
            jnp.where(bit == 0, self.total, self.others[0]).astype(F32),
            jnp.where(bit == 0, self.others[0], self.total).astype(F32),
        )


class Whole(Piece):
    def over(self):
        half, width = self.size()

        def sums(at, sources, results):
            del at
            for slot in range(2):
                for high in range(2):
                    rows = slice(high * half, (high + 1) * half)
                    results[0][slot, rows] = self.sum_of(sources, 1, slot, high).astype(BF)
                    results[1][slot, rows] = self.sum_of(sources, 0, slot, high).astype(BF)

        def after(found):
            self.across, self.low = over_y(found[0]), found[1]
            return [self.across]

        return self.sources(), [((2, 2 * half, width), BF)] * 2, sums, after

    def along(self):
        def sums(at, sources, results):
            del at
            results[0][...] = (wide(sources[0]) + wide(sources[1])).astype(BF)

        def after(found):
            self.total = lax.psum(found[0], "dp")
            return []

        return (self.low, self.across), [(self.low.shape, BF)], sums, after

    def tasks(self):
        return [self.over, self.along]

    def result(self, bit):
        del bit
        return self.total[0].astype(F32), self.total[1].astype(F32)


class Small:
    def __init__(self, rows):
        self.mine, self.other = rows, over_core(rows)

    def add(self, quarter_bit, mine, other, result):
        rows, width = mine.shape
        lanes = width // 4
        if not quarter_bit:
            result[...] = mine[...] + other[...]
            return
        for base in range(0, rows, SMALL_ROWS):
            result[base : base + 6] = mine[base : base + 6] + other[base : base + 6]
            for quarter in range(4):
                own, partner = base + 6 + quarter, base + 6 + (quarter ^ quarter_bit)
                result[own : own + 1] = mine[own : own + 1] + other[partner : partner + 1]
            tail = other[base + 8 : base + SMALL_ROWS]
            if quarter_bit == 2:
                moved = pltpu.roll(tail, 2 * lanes, 1)
            else:
                lane = lax.broadcasted_iota(jnp.int32, tail.shape, 1)
                moved = jnp.where(
                    lane % (2 * lanes) < lanes, pltpu.roll(tail, 3 * lanes, 1), pltpu.roll(tail, lanes, 1)
                )
            result[base + 10 : base + SMALL_ROWS] = mine[base + 10 : base + SMALL_ROWS] + moved[2:]

    def step(self, quarter_bit, move):
        rows, width = self.mine.shape

        def sums(at, sources, results):
            del at
            self.add(quarter_bit, *sources, results[0])

        def after(found):
            self.mine = found[0]
            self.other = move(self.mine)
            return [self.other]

        return (self.mine, self.other), [((rows, width), F32)], sums, after

    def last(self):
        rows, width = self.mine.shape
        layers, lanes = rows // SMALL_ROWS, width // 4

        def sums(at, sources, results):
            del at
            self.add(2, *sources, results[9])
            total = results[9][...]
            for layer in range(layers):
                base = SMALL_ROWS * (layers - 1 - layer)
                for item in range(7):
                    results[item][layer : layer + 1] = total[base + item : base + item + 1]
                results[7][layer] = total[base + 10 : base + 13, :lanes]
                turned = total[base + 13 : base + 15, :lanes]
                results[8][layer] = jnp.concatenate(
                    [
                        turned[:, at : at + HALF] + turned[:, at + HALF : at + HEAD_DIM]
                        for at in range(0, lanes, HEAD_DIM)
                    ],
                    axis=1,
                )

        def after(found):
            self.found = found
            return []

        shapes = [((layers, width), F32)] * 7 + [((layers, 3, lanes), F32), ((layers, 2, lanes // 2), F32)]
        shapes.append(((rows, width), F32))
        return (self.mine, self.other), shapes, sums, after

    def tasks(self):
        bits = lax.axis_size("dp").bit_length() - 1
        moves = [partial(over_bit, bit=bit) for bit in (*range(1, bits), 0)] + [over_y]
        quarters = [1] + [0] * bits
        return [partial(self.step, *item) for item in zip(quarters, moves)] + [self.last]


def attention_outputs(x_bit, pieces):
    _, width = pieces[0].total.shape
    inner = pieces[0].total.shape[0] // 2
    layers = len(pieces)

    def body(numbers, inputs, _, results, __):
        for layer in reversed(range(layers)):
            mine, other = inputs[2 * layer : 2 * layer + 2]
            first = jnp.where(numbers[0] == 0, mine[...], other[...]).astype(F32)
            second = jnp.where(numbers[0] == 0, other[...], mine[...]).astype(F32)
            results[0][layer, 0] = first[:inner]
            results[0][layer, 1] = first[inner:]
            results[0][layer, 2] = second[:inner]
            results[0].leave(layer)
            results[1][layer] = second[inner:]
            results[1].leave(layer)

    items = [item for piece in pieces for item in (piece.total, piece.others[0])]
    return staged(
        body, "attention_outputs", 0, x_bit, items, (),
        (jax.ShapeDtypeStruct((layers, 3, inner, width), F32), jax.ShapeDtypeStruct((layers, inner, width), F32)),
    )


def over_bits(values, mask):
    size = lax.axis_size("dp")
    return lax.ppermute(values, "dp", [(at, at ^ mask) for at in range(size)])


def over_both(values):
    return lax.ppermute(values, "tensor", [(at, at ^ 3) for at in range(4)])


class FarFetch:
    def __init__(self, half):
        self.mine = over_y(half)

    def turn(self, hold):
        self.mine, _ = lax.optimization_barrier((self.mine, hold))
        self.other = over_bit(self.mine, 0)
        self.mine_core = over_core(self.mine)

    def end(self, hold):
        self.other, _ = lax.optimization_barrier((self.other, hold))
        self.found = (self.mine, self.other, self.mine_core, over_core(self.other))


def body(
    tokens,
    out_grad,
    image_lengths,
    norm1_gain,
    norm1_bias,
    qkv_weight,
    qkv_bias,
    rope_freqs,
    out_weight,
    out_bias,
    norm2_gain,
    norm2_bias,
    up_weight,
    up_bias,
    down_weight,
    down_bias,
):
    count, width = tokens.shape
    inner = qkv_weight.shape[3]
    heads = inner // HEAD_DIM
    me = lax.axis_index("tensor")
    xbit = lax.axis_index("dp") & 1
    x_bit = jnp.stack([xbit, xbit]).astype(jnp.int32)
    x_bit_plain = jnp.stack([xbit, jnp.zeros_like(xbit)]).astype(jnp.int32)

    small = jnp.concatenate(
        [qkv_bias.reshape(LAYERS, -1), rope_freqs.reshape(LAYERS, -1), up_bias], axis=1
    )
    near_small, far_small = (small, over_core(small)), (over_y(small), over_both(small))

    lengths = lax.dynamic_index_in_dim(image_lengths, me // 2, 0, keepdims=False)
    half_at = me % 2
    position = jnp.arange(count, dtype=jnp.int32)
    segment, row_at, column_at = places_at(lengths, position + half_at * count)
    segment_other, _, _ = places_at(lengths, position + (1 - half_at) * count)
    here_segment = segment[:, None].astype(F32)
    all_segments = jnp.concatenate([segment, segment_other])[None, :].astype(F32)
    places = jnp.stack([row_at, column_at], axis=1).astype(F32)

    qkv_turned = jnp.swapaxes(qkv_weight, 2, 3)
    near_att, far_att, near_mlp, far_mlp = [], [], [], []

    def fetch_att(layer, gates=()):
        packed, half = pack(layer, x_bit, qkv_turned, out_weight[:, None], 2, gates)
        near_att.append((packed, over_core(packed)))
        far_att.append(FarFetch(half))

    def fetch_mlp(layer, gates=()):
        both, half = pack(layer, x_bit, up_weight[:, None], down_weight[:, None], 1, gates)
        near_mlp.append((both, over_core(both)))
        far_mlp.append(FarFetch(half[0]))

    current = tokens
    kept_layers = []
    cosines, sines = [[] for _ in range(LAYERS)], [[] for _ in range(LAYERS)]
    before = ()
    fetch_att(0)
    for l in range(LAYERS):
        inputs = current
        gain, shift = norm1_gain[l : l + 1], norm1_bias[l : l + 1]
        queries, keeps, comes, mixes, spreads, exps = [], [], [], [], [], []

        def project(side, source, weights):
            nonlocal before
            found = qkv_part(
                side == 0, l, x_bit, source, gain, shift, (near_small, far_small)[side], places, weights, before
            )
            before = (found[0],)
            queries.append(found[0])
            keeps.append(found[1])
            comes.append(over_core(found[2]))
            cosines[l].append(found[3])
            sines[l].append(found[4])
            return found

        def mix(side):
            nonlocal before
            found = attend(queries[side], keeps[side], comes[side], here_segment, all_segments, x_bit, before)
            before = (found[0],)
            mixes.append(found[0])
            spreads.append(found[1])
            exps.append(found[2])

        normed = project(0, inputs, near_att[l])[5]
        if l:
            far_mlp[l].turn(queries[0])
        if l == 0:
            fetch_mlp(0, before + far_small)
            before = (near_mlp[0][0],)
            far_att[0].turn(near_mlp[0][0])
            mix(0)
            fetch_att(1, before)
            before = (near_att[1][0],)
            far_att[0].end(mixes[0])
            far_mlp[0].turn(mixes[0])
            project(1, normed, far_att[0].found)
            mix(1)
            fetch_mlp(1, before)
            before = (near_mlp[1][0],)
            far_att[1].turn(mixes[1])
            far_mlp[0].end(mixes[1])
        else:
            project(1, normed, far_att[l].found)
            mix(0)
            mix(1)
            far_mlp[l].end(mixes[1])
        middle, normed_mlp, active_near, slope_near, total = mlp_near(
            l, x_bit, inputs, mixes[0], mixes[1], out_bias[l : l + 1], norm2_gain[l : l + 1], norm2_bias[l : l + 1],
            near_small, down_bias[l : l + 1], near_att[l] + far_att[l].found, near_mlp[l], before,
        )
        active_far, slope_far, current = mlp_far(
            l, x_bit, normed_mlp, total, far_small, far_mlp[l].found, BF if l == LAYERS - 1 else F32
        )
        before = (current,)
        if l == 0:
            far_att[1].end(middle)
        kept_layers.append(
            (inputs, normed, queries, keeps, comes, mixes, spreads, exps, middle, normed_mlp, (active_near, active_far), (slope_near, slope_far))
        )
    activations = current

    gradient = out_grad
    small_rows = []
    summed = [None] * LAYERS
    waiting = []
    todo = []
    clock = 0
    latest = []
    here = lax.axis_index("dp").reshape(1).astype(jnp.int32)

    def ran(found):
        latest[:] = found[:1]
        return found

    def wait_until(arrays, when):
        waiting.append((when, arrays))

    def gates_now():
        nonlocal clock
        clock += 1
        due = [array for when, arrays in waiting if when <= clock for array in arrays]
        waiting[:] = [item for item in waiting if item[0] > clock]
        turn = [entry for entry in todo if entry[0] == clock]
        todo[:] = [entry for entry in todo if entry[0] != clock]
        if not turn:
            return due + latest
        tasks = [step() for _, _, step in turn]
        found = run_tasks(here, [task[:3] for task in tasks], due + latest)
        for (_, length, _), task, given in zip(turn, tasks, found):
            wait_until(task[3](given), clock + length)
        latest[:] = found[0][:1]
        return latest

    def plan(piece, base, table):
        start, length = 0, 1
        for at, step in enumerate(piece.tasks()):
            start, length = table[at] if at < len(table) else (start + length, 1)
            todo.append((base + start, length, step))

    for l in reversed(range(LAYERS)):
        (inputs, normed, queries, keeps, comes, mixes, spreads, exps, middle, normed_mlp, active, slope) = kept_layers[l]
        att = (near_att[l], far_att[l].found)
        pieces = [Piece(), Piece()]
        tables = PLANS[l > 0]
        for piece, table in zip(pieces, tables):
            plan(piece, clock, table)
        found, rest = mlp_back(
            x_bit, gradient, normed_mlp, middle, norm2_gain[l : l + 1], active, slope, near_mlp[l],
            far_mlp[l].found, gates_now(),
        )
        ran(rest)
        up_bias_grad, sums2, grad_middle, incoming = rest
        wait_until(pieces[0].begin(found), clock + tables[0][0][0] - 1)
        backs = attend_back(
            x_bit, incoming,
            [(queries[side], keeps[side], comes[side], mixes[side], spreads[side], exps[side]) for side in range(2)],
            *att, gates_now(),
        )
        ran(backs[0])
        sides = [
            (back[0], back[1], over_core(back[2]), over_core(back[3]), queries[side], keeps[side], cosines[l][side], sines[l][side], mixes[side])
            for side, back in enumerate(backs)
        ]
        found, rest = qkv_back(
            x_bit, normed, incoming, places, sides, *att, norm1_gain[l : l + 1], inputs, grad_middle,
            [sums2, up_bias_grad] + small_rows, gates_now(),
        )
        ran(rest)
        rows, gradient = rest
        small_rows = [rows]
        wait_until(pieces[1].begin(found), clock + tables[1][0][0] - 3)
        summed[l] = pieces

    little = Small(small_rows[0])
    wait_until([little.other], clock + SMALL_PLAN[0][0])
    plan(little, clock, SMALL_PLAN)
    while todo:
        gates_now()
    gain1, shift1, bias_out, gain2, shift2, bias_down, bias_up, bias_qkv, turns = little.found[:9]
    grad_qkv, grad_out = attention_outputs(x_bit, [summed[l][1] for l in range(LAYERS)])
    grad_up, grad_down = zip(*(summed[l][0].result(xbit) for l in range(LAYERS)))
    return (
        activations,
        gradient,
        gain1,
        shift1,
        jnp.swapaxes(grad_qkv, 2, 3),
        bias_qkv,
        turns,
        grad_out,
        bias_out,
        gain2,
        shift2,
        jnp.stack(grad_up),
        bias_up,
        jnp.stack(grad_down),
        bias_down,
    )


def solution(mesh):
    in_specs = (
        P(("dp", "tensor"), None),
        P(("dp", "tensor"), None),
        P("dp", None),
        P(),
        P(),
        P(None, None, None, "tensor"),
        P(None, None, "tensor"),
        P(None, None, "tensor"),
        P(None, "tensor", None),
        P(),
        P(),
        P(),
        P(None, None, "tensor"),
        P(None, "tensor"),
        P(None, "tensor", None),
        P(),
    )
    out_specs = (
        P(("dp", "tensor"), None),
        P(("dp", "tensor"), None),
        P(),
        P(),
        P(None, None, None, "tensor"),
        P(None, None, "tensor"),
        P(None, None, "tensor"),
        P(None, "tensor", None),
        P(),
        P(),
        P(),
        P(None, None, "tensor"),
        P(None, "tensor"),
        P(None, "tensor", None),
        P(),
    )
    return jax.shard_map(body, mesh=mesh, in_specs=in_specs, out_specs=out_specs, check_vma=False)
```

```python
from functools import partial

import jax
import jax.numpy as jnp
from jax import lax
from jax.experimental import pallas as pl
from jax.experimental.pallas import tpu as pltpu
from jax.sharding import PartitionSpec as P

HEAD_DIM = 64
LEN = 832
SIDE_S = 14
SIDE_M = 20
SIDE_L = 24
MAX_IMAGES = 4
LAYERS = 2

EPS = 1e-06
NEGATIVE = -1000000000.0
BF = jnp.bfloat16
F32 = jnp.float32

CORE = [(0, 1), (1, 0), (2, 3), (3, 2)]
ACROSS = [(0, 2), (2, 0), (1, 3), (3, 1)]


def over_core(values):
    return lax.ppermute(values, "tensor", CORE)


def over_y(values):
    return lax.ppermute(values, "tensor", ACROSS)


def over_bit(values, bit):
    size = lax.axis_size("dp")
    return lax.ppermute(values, "dp", [(at, at ^ (1 << bit)) for at in range(size)])


def places_at(lengths, position):
    ends = jnp.cumsum(lengths)
    starts = ends - lengths
    segment = jnp.sum((position[:, None] >= ends[None, :]).astype(jnp.int32), axis=1)
    belongs = segment[:, None] == jnp.arange(MAX_IMAGES, dtype=jnp.int32)[None, :]
    begin_at = jnp.sum(jnp.where(belongs, starts[None, :], 0), axis=1)
    size = jnp.sum(jnp.where(belongs, lengths[None, :], 0), axis=1)
    side = jnp.where(
        size == SIDE_S * SIDE_S, SIDE_S, jnp.where(size == SIDE_M * SIDE_M, SIDE_M, SIDE_L)
    ).astype(jnp.int32)
    offset = position - begin_at
    inside = segment < MAX_IMAGES
    row_at = jnp.where(inside, offset // side, 0)
    column_at = jnp.where(inside, offset % side, 0)
    return segment, row_at, column_at


PLANS = (
    (
        ((3, 2), (5, 1), (6, 1), (7, 1), (8, 1), (9, 1), (10, 9)),
        ((4, 1), (5, 1), (6, 1), (7, 1), (8, 1), (9, 1), (10, 9)),
    ),
    (
        ((3, 1), (4, 1), (5, 1), (6, 1), (7, 1), (8, 1), (9, 1)),
        ((5, 1), (6, 1), (7, 1), (8, 1), (9, 1), (10, 1), (11, 1)),
    ),
)
SMALL_PLAN = ((3, 1), (4, 1), (5, 1), (6, 1), (7, 1))
VMEM_BYTES = 58 * 2**20
PARAMS = pltpu.CompilerParams(vmem_limit_bytes=VMEM_BYTES)
WHOLE = pl.BlockSpec(memory_space=pltpu.VMEM)
PLACE = pl.BlockSpec(memory_space=pl.ANY)
SCALAR = pl.BlockSpec(memory_space=pltpu.SMEM)
HALF = HEAD_DIM // 2
SIDE_ROWS = 32
SMALL_ROWS = 16


def dot(left, right, on_left, on_right):
    return lax.dot_general(
        left, right, (((on_left,), (on_right,)), ((), ())), preferred_element_type=F32
    )


def norm_parts(values):
    average = jnp.mean(values, axis=-1, keepdims=True)
    centred = values - average
    variance = jnp.mean(centred * centred, axis=-1, keepdims=True)
    inverse = lax.rsqrt(variance + EPS)
    return centred * inverse, inverse


def norm_back(values, gain, incoming):
    xhat, inverse = norm_parts(values)
    grad_gain = jnp.sum(incoming * xhat, axis=0, keepdims=True)
    grad_shift = jnp.sum(incoming, axis=0, keepdims=True)
    scaled = incoming * gain
    through = inverse * (
        scaled
        - jnp.mean(scaled, axis=-1, keepdims=True)
        - xhat * jnp.mean(scaled * xhat, axis=-1, keepdims=True)
    )
    return through, grad_gain, grad_shift


def first_half(shape):
    return lax.broadcasted_iota(jnp.int32, shape, 1) % HEAD_DIM < HALF


def swap(values):
    width = values.shape[1]
    return jnp.where(
        first_half(values.shape),
        pltpu.roll(values, width - HALF, 1),
        pltpu.roll(values, HALF, 1),
    )


def one_head(values, head):
    lane = lax.broadcasted_iota(jnp.int32, values.shape, 1)
    return jnp.where((lane < HEAD_DIM) == (head == 0), values, jnp.zeros_like(values))


def join_heads(first, second):
    lane = lax.broadcasted_iota(jnp.int32, first.shape, 1)
    return jnp.where(lane < HEAD_DIM, first, second)


class Held:
    def __init__(self, source, buffer, sem):
        self.copy, self.buffer, self.done = pltpu.make_async_copy(source, buffer, sem), buffer, False
        self.shape, self.dtype = buffer.shape, buffer.dtype
        self.copy.start()

    def wait(self):
        if not self.done:
            self.copy.wait()
            self.done = True

    def __getitem__(self, at):
        self.wait()
        return self.buffer[at]


class Given:
    def __init__(self, target, buffer, sems):
        self.target, self.buffer, self.sems, self.copies = target, buffer, sems, []

    def __setitem__(self, at, values):
        self.buffer[at] = values

    def __getitem__(self, at):
        return self.buffer[at]

    def leave(self, at=None):
        source, target = self.buffer, self.target
        if at is not None:
            source, target = source.at[at], target.at[at]
        self.copies.append(pltpu.make_async_copy(source, target, self.sems.at[len(self.copies)]))
        self.copies[-1].start()


PIECES_OUT = 6


def staged(body, name, flops, scalars, inputs, raws, outs, raw_outs=(), scratch=(), gates=()):
    counts = [len(inputs), len(raws), len(gates), len(outs), len(raw_outs)]

    def kernel(numbers, *refs):
        groups = []
        for count in counts:
            groups.append(refs[:count])
            refs = refs[count:]
        sources, plain, _, targets, plain_targets = groups
        in_buffers, out_buffers, rest = refs[: counts[0]], refs[counts[0] : counts[0] + counts[3]], refs[counts[0] + counts[3] :]
        in_sems, out_sems, rest = rest[0], rest[1], rest[2:]
        held = [Held(*item, in_sems.at[at]) for at, item in enumerate(zip(sources, in_buffers))]
        given = [Given(*item, out_sems.at[at]) for at, item in enumerate(zip(targets, out_buffers))]
        body(numbers, held, plain, given, plain_targets, *rest)
        for item in held:
            item.wait()
        for item in given:
            if not item.copies:
                item.leave()
        for item in given:
            for copy in item.copies:
                copy.wait()

    return pl.pallas_call(
        kernel,
        out_shape=list(outs) + list(raw_outs),
        in_specs=[SCALAR] + [PLACE] * sum(counts[:3]),
        out_specs=[PLACE] * sum(counts[3:]),
        scratch_shapes=[pltpu.VMEM(item.shape, item.dtype) for item in list(inputs) + list(outs)]
        + [pltpu.SemaphoreType.DMA((max(counts[0], 1),)), pltpu.SemaphoreType.DMA((max(counts[3], 1), PIECES_OUT))]
        + list(scratch),
        compiler_params=PARAMS,
        name=name,
        cost_estimate=pl.CostEstimate(flops=flops // 8, bytes_accessed=2**20, transcendentals=0),
    )(scalars, *inputs, *raws, *gates)


def fetch(pairs, sems):
    copies = [pltpu.make_async_copy(source, target, sems.at[at]) for at, (source, target) in enumerate(pairs)]
    for copy in copies:
        copy.start()
    return copies


def att_pairs(near, refs, into, xbit, parts):
    inner = into.shape[1] // 2
    low, high = pl.ds(0, inner), pl.ds(inner, inner)
    if near:
        return [(refs[0].at[pl.ds(0, parts)], into.at[pl.ds(0, parts), low]), (refs[1].at[pl.ds(0, parts)], into.at[pl.ds(0, parts), high])]
    mine, other = pl.ds(2 * xbit, 2), pl.ds(2 - 2 * xbit, 2)
    return [
        (refs[0], into.at[mine, low]),
        (refs[1], into.at[other, low]),
        (refs[2], into.at[mine, high]),
        (refs[3], into.at[other, high]),
    ]


def mlp_pairs(near, refs, into, xbit):
    if near:
        return [(ref, into.at[quarter]) for quarter, ref in enumerate(refs)]
    slots = ((0, xbit), (0, 1 - xbit), (1, xbit), (1, 1 - xbit))
    return [(ref, into.at[quarter, slot]) for ref, (quarter, slot) in zip(refs, slots)]


def pack(layer, x_bit, first, second, cut, gates=()):
    _, rows, width, inner = first.shape
    more = second.shape[1]

    def body(numbers, _, raws, __, targets, held, sems):
        whole, half = targets
        for copy in fetch(
            [(raws[0].at[layer], held.at[pl.ds(0, rows)]), (raws[1].at[layer], held.at[pl.ds(rows, more)])], sems
        ):
            copy.wait()
        copies = [
            pltpu.make_async_copy(held.at[pl.ds(cut * numbers[0], cut)], half, sems.at[2]),
            pltpu.make_async_copy(held, whole, sems.at[3]),
        ]
        for copy in copies:
            copy.start()
        for copy in copies:
            copy.wait()

    return staged(
        body, "pack", 0, x_bit, (), (first, second), (),
        (
            jax.ShapeDtypeStruct((rows + more, width, inner), BF),
            jax.ShapeDtypeStruct((cut, width, inner), BF),
        ),
        (pltpu.VMEM((rows + more, width, inner), BF), pltpu.SemaphoreType.DMA((4,))), gates,
    )


def angle_tables(freqs, places):
    steps = lax.broadcasted_iota(jnp.int32, (SIDE_ROWS, 1), 0).astype(F32)
    found = []
    for axis in range(2):
        terms = steps * freqs[axis]
        table = jnp.concatenate([jnp.cos(terms), jnp.sin(terms)], axis=1)
        at = places[:, axis : axis + 1]
        column = lax.broadcasted_iota(jnp.int32, (places.shape[0], SIDE_ROWS), 1).astype(F32)
        chosen = lax.dot_general(
            (column == at).astype(F32), table, (((1,), (0,)), ((), ())),
            precision=lax.Precision.HIGHEST, preferred_element_type=F32,
        )
        width = terms.shape[1]
        found.append((chosen[:, :width], chosen[:, width:]))
    (row_cos, row_sin), (col_cos, col_sin) = found
    cosine = row_cos * col_cos - row_sin * col_sin
    sine = row_sin * col_cos + row_cos * col_sin
    return cosine, jnp.where(first_half(sine.shape), -sine, sine)


def qkv_part(near, layer, x_bit, source, gain, shift, small, places, weights, gates=()):
    count, width = source.shape
    inner = weights[0].shape[1]

    def body(numbers, inputs, raws, results, _, held, sems):
        gain, shift, places, first, second, source = inputs
        query, kept, sent, cosine, sine = results[:5]
        copies = fetch(att_pairs(near, raws, held, numbers[0], 3), sems)
        both = [item[layer : layer + 1] for item in (first, second)]
        bias = [
            jnp.concatenate([item[:, part * inner : (part + 1) * inner] for item in both], axis=1)
            for part in range(3)
        ]
        freqs = []
        for axis in range(2):
            begin = 3 * inner + axis * (inner // 2)
            pieces = [item[:, at : at + HALF] for item in both for at in range(begin, begin + inner // 2, HALF)]
            freqs.append(jnp.concatenate([piece for piece in pieces for _ in range(2)], axis=1))
        cosine[...], sine[...] = angle_tables(freqs, places[...])
        cosine.leave()
        sine.leave()
        if near:
            xhat, _ = norm_parts(source[...].astype(F32))
            normed = (xhat * gain[...] + shift[...]).astype(BF)
            results[5][...] = normed
            results[5].leave()
        else:
            normed = source[...]
        for copy in copies:
            copy.wait()
        for part in (1, 2, 0):
            values = dot(normed, held[part], 1, 1) + bias[part]
            if part < 2:
                values = values * cosine[...] + swap(values) * sine[...]
            if part == 0:
                query[...] = (values * HEAD_DIM**-0.5).astype(BF)
            else:
                kept[part - 1] = values.astype(BF)
                sent[part - 1] = pltpu.roll(values, inner, 1).astype(BF)
                sent.leave(part - 1)

    pair = jax.ShapeDtypeStruct((2, count, 2 * inner), BF)
    table = jax.ShapeDtypeStruct((count, 2 * inner), F32)
    outs = [jax.ShapeDtypeStruct((count, 2 * inner), BF), pair, pair, table, table]
    if near:
        outs.append(jax.ShapeDtypeStruct((count, width), BF))
    return staged(
        body, "qkv_near" if near else "qkv_far", 2 * count * width * 6 * inner, x_bit,
        (gain, shift, places, *small, source), weights, outs,
        scratch=(pltpu.VMEM((4, 2 * inner, width), BF), pltpu.SemaphoreType.DMA((len(weights),))), gates=gates,
    )


def attend(query, kept, came, here, there, number, gates=()):
    count, width = query.shape
    heads = width // HEAD_DIM

    def body(_, inputs, __, results, ___):
        query, kept, here, came, there = inputs
        mixed, spread, exps = results
        allowed = here[...] == there[...]
        for pair in range(heads // 2):
            lanes = slice(2 * HEAD_DIM * pair, 2 * HEAD_DIM * (pair + 1))
            keys = jnp.concatenate([kept[0, :, lanes], came[0, :, lanes]], axis=0)
            values = jnp.concatenate([kept[1, :, lanes], came[1, :, lanes]], axis=0)
            outs, inverses = [], []
            for head in range(2):
                scores = dot(one_head(query[:, lanes], head), keys, 1, 1)
                scores = jnp.where(allowed, scores, NEGATIVE)
                highest = jnp.max(scores, axis=1, keepdims=True)
                raised = jnp.exp(scores - highest)
                inverse = 1.0 / jnp.sum(raised, axis=1, keepdims=True)
                low = raised.astype(BF)
                exps[2 * pair + head] = low
                exps.leave(2 * pair + head)
                outs.append(dot(low, values, 1, 0) * inverse)
                inverses.append(jnp.broadcast_to(inverse, outs[0].shape))
            mixed[:, lanes] = join_heads(*outs).astype(BF)
            spread[:, lanes] = join_heads(*inverses)

    return staged(
        body, "attend", 8 * count * width * 768, number, (query, kept, here, came, there), (),
        (
            jax.ShapeDtypeStruct((count, width), BF),
            jax.ShapeDtypeStruct((count, width), F32),
            jax.ShapeDtypeStruct((heads, count, 2 * count), BF),
        ),
        gates=gates,
    )


def gelu_parts(pre):
    size = jnp.abs(pre)
    ratio = 1.0 / (1.0 + 0.3275911 * (0.5**0.5) * size)
    bell = jnp.exp(-0.5 * pre * pre)
    poly = ((((0.5 * 1.061405429 * ratio - 0.5 * 1.453152027) * ratio + 0.5 * 1.421413741) * ratio - 0.5 * 0.284496736) * ratio + 0.5 * 0.254829592) * ratio
    below = poly * bell
    normal = jnp.where(pre < 0, below, 1.0 - below)
    return pre * normal, normal + pre * (bell * 0.3989422804014327)


def feed(quarter, normed, held, up_bias, active, slope):
    value, rate = gelu_parts(dot(normed, held[quarter, 0], 1, 0) + up_bias[quarter])
    low = value.astype(BF)
    active[quarter] = low
    active.leave(quarter)
    slope[quarter] = rate.astype(BF)
    slope.leave(quarter)
    return dot(low, held[quarter, 1], 1, 0)


def mlp_near(layer, x_bit, inputs, mixed_near, mixed_far, out_bias, gain, shift, small, down_bias, outs, weights, gates=()):
    count, width = inputs.shape
    hidden = weights[0].shape[2]
    inner = outs[0].shape[1]

    def body(numbers, held_inputs, raws, results, _, held_out, held, sems):
        mixed_near, mixed_far, inputs, out_bias, gain, shift, first, second, down_bias = held_inputs
        up_bias = [item[layer : layer + 1, width:] for item in (first, second)]
        middle, normed_out, active, slope, total = results
        xbit = numbers[0]
        copies = fetch(
            [
                (raws[0].at[3], held_out.at[0]),
                (raws[1].at[3], held_out.at[1]),
                (raws[2].at[1], held_out.at[2 + 2 * (1 - xbit)]),
                (raws[3].at[1], held_out.at[2 + 2 * xbit]),
                (raws[4].at[1], held_out.at[3 + 2 * (1 - xbit)]),
                (raws[5].at[1], held_out.at[3 + 2 * xbit]),
            ]
            + mlp_pairs(True, raws[6:], held, xbit),
            sems,
        )
        for copy in copies[:6]:
            copy.wait()
        centre = dot(mixed_near[...], jnp.concatenate([held_out[0], held_out[1]], axis=0), 1, 0)
        centre = centre + dot(mixed_far[...], jnp.concatenate([held_out[2], held_out[3]], axis=0), 1, 0)
        centre = centre + inputs[...].astype(F32) + out_bias[...]
        middle[...] = centre
        middle.leave()
        xhat, _ = norm_parts(centre)
        normed = (xhat * gain[...] + shift[...]).astype(BF)
        normed_out[...] = normed
        normed_out.leave()
        gathered = centre + down_bias[...]
        for quarter in range(2):
            copies[6 + quarter].wait()
            gathered = gathered + feed(quarter, normed, held, up_bias, active, slope)
        total[...] = gathered

    kept = jax.ShapeDtypeStruct((2, count, hidden), BF)
    full = jax.ShapeDtypeStruct((count, width), F32)
    return staged(
        body, "mlp_near", 10 * count * width * width, x_bit,
        (mixed_near, mixed_far, inputs, out_bias, gain, shift, *small, down_bias), tuple(outs) + tuple(weights),
        (full, jax.ShapeDtypeStruct((count, width), BF), kept, kept, full),
        scratch=(
            pltpu.VMEM((6, inner, width), BF),
            pltpu.VMEM((2, 2, width, hidden), BF),
            pltpu.SemaphoreType.DMA((8,)),
        ),
        gates=gates,
    )


def mlp_far(layer, x_bit, normed, total, small, weights, dtype, gates=()):
    count, width = normed.shape
    hidden = weights[0].shape[1]

    def body(numbers, inputs, raws, results, _, held, sems):
        normed, first, second, total = inputs
        up_bias = [item[layer : layer + 1, width:] for item in (first, second)]
        active, slope, result = results
        copies = fetch(mlp_pairs(False, raws, held, numbers[0]), sems)
        gathered = None
        for quarter in range(2):
            for copy in copies[2 * quarter : 2 * quarter + 2]:
                copy.wait()
            term = feed(quarter, normed[...], held, up_bias, active, slope)
            gathered = total[...] + term if gathered is None else gathered + term
        result[...] = gathered.astype(dtype)

    kept = jax.ShapeDtypeStruct((2, count, hidden), BF)
    return staged(
        body, "mlp_far", 8 * count * width * width, x_bit, (normed, *small, total), weights,
        (kept, kept, jax.ShapeDtypeStruct((count, width), dtype)),
        scratch=(pltpu.VMEM((2, 2, width, hidden), BF), pltpu.SemaphoreType.DMA((4,))), gates=gates,
    )


def mlp_back(x_bit, gradient, normed, middle, gain, active, slope, near, far, gates=()):
    count, width = normed.shape
    hidden = active[0].shape[2]

    def body(numbers, inputs, raws, results, grads, held, ready, sems, out_sems):
        gradient, active_far, slope_far, normed, active_near, slope_near, gain, middle = inputs
        bias_grad, sums, grad_middle, low_middle = results
        xbit, up_slot = numbers[0], numbers[1]
        targets = (grads[0:1], grads[1:5], grads[5:6], grads[6:10])
        copies = fetch(
            mlp_pairs(False, raws[2:], held.at[pl.ds(2, 2)], xbit) + mlp_pairs(True, raws[:2], held.at[pl.ds(0, 2)], xbit), sems
        )
        needed = ((copies[4],), (copies[5],), copies[0:2], copies[2:4])
        leaving = []

        def leave(quarter, kind, slot, values):
            ready[quarter, kind] = values.astype(BF)
            rows = targets[quarter][0].shape[1]
            for at, target in enumerate(targets[quarter]):
                copy = pltpu.make_async_copy(
                    ready.at[quarter, kind, pl.ds(at * rows, rows)], target.at[slot], out_sems.at[len(leaving)]
                )
                copy.start()
                leaving.append(copy)

        incoming = gradient[...].astype(F32)
        low = incoming.astype(BF)
        gathered = None
        for quarter in (3, 2, 1, 0):
            active, slope = (active_near, slope_near) if quarter < 2 else (active_far, slope_far)
            leave(quarter, 0, 1 - up_slot, dot(active[quarter % 2], low, 0, 0))
            for copy in needed[quarter]:
                copy.wait()
            inside = dot(low, held[quarter, 1], 1, 1) * slope[quarter % 2].astype(F32)
            low_inside = inside.astype(BF)
            bias_grad[quarter : quarter + 1] = jnp.sum(low_inside.astype(F32), axis=0, keepdims=True)
            leave(quarter, 1, up_slot, dot(normed[...], low_inside, 0, 0))
            term = dot(low_inside, held[quarter, 0], 1, 1)
            gathered = term if gathered is None else gathered + term
        through, grad_gain, grad_shift = norm_back(middle[...], gain[...], gathered)
        result = incoming + through
        grad_middle[...] = result
        grad_middle.leave()
        low_result = result.astype(BF)
        low_middle[...] = low_result
        low_middle.leave()
        sums[0:1] = grad_gain
        sums[1:2] = grad_shift
        sums[2:3] = jnp.sum(low_result.astype(F32), axis=0, keepdims=True)
        sums[3:4] = jnp.sum(low.astype(F32), axis=0, keepdims=True)
        for copy in leaving:
            copy.wait()

    whole = jax.ShapeDtypeStruct((2, width, hidden), BF)
    part = jax.ShapeDtypeStruct((2, width // 4, hidden), BF)
    outs = [
        jax.ShapeDtypeStruct((4, hidden), F32),
        jax.ShapeDtypeStruct((4, width), F32),
        jax.ShapeDtypeStruct((count, width), F32),
        jax.ShapeDtypeStruct((count, width), BF),
    ]
    found = staged(
        body, "mlp_back", 32 * count * width * width, x_bit,
        (gradient, active[1], slope[1], normed, active[0], slope[0], gain, middle), tuple(near) + tuple(far), outs,
        ([whole] + [part] * 4) * 2,
        (
            pltpu.VMEM((4, 2, width, hidden), BF),
            pltpu.VMEM((4, 2, width, hidden), BF),
            pltpu.SemaphoreType.DMA((6,)),
            pltpu.SemaphoreType.DMA((20,)),
        ),
        gates,
    )
    return (found[4], found[5:9], found[9], found[10:14]), found[:4]


def attend_back(x_bit, incoming, sides, near, far, gates=()):
    count, width = sides[0][0].shape
    pairs = width // (2 * HEAD_DIM)
    inner, full = near[0].shape[1:]

    def body(numbers, inputs, raws, results, _, held, sems):
        incoming, xbit = inputs[0], numbers[0]
        copies = fetch(
            [
                (raws[0].at[3], held.at[0]),
                (raws[1].at[3], held.at[1]),
                (raws[2].at[1], held.at[2 + 2 * (1 - xbit)]),
                (raws[3].at[1], held.at[2 + 2 * xbit]),
                (raws[4].at[1], held.at[3 + 2 * (1 - xbit)]),
                (raws[5].at[1], held.at[3 + 2 * xbit]),
            ],
            sems,
        )
        for copy in copies:
            copy.wait()
        for side in (0, 1):
            mixed, spread, kept, came, query, exps = inputs[1 + 6 * side : 7 + 6 * side]
            grad_query, grad_kept, *grad_sent = results[4 * side : 4 * side + 4]
            both = jnp.concatenate([held[2 * side], held[2 * side + 1]], axis=0)
            scaled = dot(incoming[...], both, 1, 1) * spread[...]
            product_all = scaled * mixed[...].astype(F32)
            low_all = scaled.astype(BF)
            for pair in range(pairs):
                lanes = slice(2 * HEAD_DIM * pair, 2 * HEAD_DIM * (pair + 1))
                keys = jnp.concatenate([kept[0, :, lanes], came[0, :, lanes]], axis=0)
                values = jnp.concatenate([kept[1, :, lanes], came[1, :, lanes]], axis=0)
                low_mixed, product = low_all[:, lanes], product_all[:, lanes]
                for_query, for_key, for_value = [], [], []
                for head in range(2):
                    raised = exps[2 * pair + head]
                    level = jnp.sum(one_head(product, head), axis=1, keepdims=True)
                    grad_probs = dot(one_head(low_mixed, head), values, 1, 1)
                    grad_scores = (raised.astype(F32) * (grad_probs - level)).astype(BF)
                    for_value.append(dot(raised, low_mixed, 0, 0))
                    for_query.append(dot(grad_scores, keys, 1, 0))
                    for_key.append(dot(grad_scores, query[:, lanes], 0, 0))
                grad_query[:, lanes] = join_heads(*for_query).astype(BF)
                for part, both_heads in enumerate((for_key, for_value)):
                    joined = join_heads(*both_heads).astype(BF)
                    grad_kept[part, :, lanes] = joined[:count]
                    grad_sent[part][:, lanes] = joined[count:]
            for item in results[4 * side : 4 * side + 4]:
                item.leave()

    shapes = [
        jax.ShapeDtypeStruct((count, width), BF),
        jax.ShapeDtypeStruct((2, count, width), BF),
        jax.ShapeDtypeStruct((count, width), BF),
        jax.ShapeDtypeStruct((count, width), BF),
    ]
    ordered = [incoming]
    for query, kept, came, mixed, spread, exps in sides:
        ordered += [mixed, spread, kept, came, query, exps]
    found = staged(
        body, "attend_back", 32 * count * width * full, x_bit, ordered, tuple(near) + tuple(far), shapes * 2,
        scratch=(pltpu.VMEM((6, inner, full), BF), pltpu.SemaphoreType.DMA((6,))),
        gates=gates,
    )
    return found[:4], found[4:]


def qkv_back(x_bit, normed, incoming, places, sides, near, far, gain, inputs_kept, grad_middle, little, gates=()):
    count, width = normed.shape
    inner = near[0].shape[1]

    def body(numbers, inputs, raws, results, grads, held, ready, sems, out_sems):
        normed, incoming, places = inputs[:3]
        gain, inputs_kept, grad_middle, sums2, up_bias_grad = inputs[21:26]
        rows_out, result = results
        earlier = inputs[26:]
        base = SMALL_ROWS * len(earlier)
        for at, item in enumerate(earlier):
            rows_out[SMALL_ROWS * at : SMALL_ROWS * (at + 1)] = item[...]
        xbit = numbers[0]
        targets = (grads[0:1], grads[1:3], grads[3:4], grads[4:6])
        copies = fetch(
            att_pairs(False, raws[2:], held.at[1], xbit, 3) + att_pairs(True, raws[:2], held.at[0], xbit, 3), sems
        )
        needed = (copies[4:], copies[:4])
        slots = (2 * xbit, 2 * xbit + 1, 2 - 2 * xbit, 3 - 2 * xbit)
        leaving = []

        def store(side, part, values):
            ready[side, part] = values.astype(BF)
            for quarter in range(2):
                rows = targets[2 * side + quarter][0].shape[1]
                for at, target in enumerate(targets[2 * side + quarter]):
                    copy = pltpu.make_async_copy(
                        ready.at[side, part, pl.ds(quarter * inner + at * rows, rows)],
                        target.at[slots[part]],
                        out_sems.at[len(leaving)],
                    )
                    copy.start()
                    leaving.append(copy)

        gathered = None
        for side in (1, 0):
            mixed, grad_query, query, grad_kept, came_key, came_value, kept, cosine, sine = inputs[3 + 9 * side : 12 + 9 * side]
            lanes = slice(2 * inner * side, 2 * inner * (side + 1))
            store(side, 3, dot(mixed[...], incoming[...], 0, 0))
            sign = jnp.where(first_half(query.shape), -1.0, 1.0)
            raw_query = grad_query[...].astype(F32)
            raw_key = grad_kept[0].astype(F32) + pltpu.roll(came_key[...].astype(F32), inner, 1)
            raw_value = grad_kept[1].astype(F32) + pltpu.roll(came_value[...].astype(F32), inner, 1)
            angle = (raw_query * swap(query[...].astype(F32)) + raw_key * swap(kept[0].astype(F32))) * sign
            for axis in range(2):
                rows_out[base + 13 + axis : base + 14 + axis, lanes] = jnp.sum(
                    angle * places[:, axis : axis + 1], axis=0, keepdims=True
                )
            cos, sin = cosine[...], sine[...]
            turned = (
                (raw_query * cos - swap(raw_query) * sin) * HEAD_DIM**-0.5,
                raw_key * cos - swap(raw_key) * sin,
                raw_value,
            )
            lows = [item.astype(BF) for item in turned]
            for part in range(3):
                rows_out[base + 10 + part : base + 11 + part, lanes] = jnp.sum(
                    lows[part].astype(F32), axis=0, keepdims=True
                )
                store(side, part, dot(lows[part], normed[...], 0, 0))
            for copy in needed[side]:
                copy.wait()
            for part in range(3):
                term = dot(lows[part], held[side, part], 1, 0)
                gathered = term if gathered is None else gathered + term
        through, grad_gain, grad_shift = norm_back(inputs_kept[...].astype(F32), gain[...], gathered)
        result[...] = grad_middle[...] + through
        rows_out[base : base + 1] = grad_gain
        rows_out[base + 1 : base + 2] = grad_shift
        rows_out[base + 2 : base + 3] = sums2[2:3]
        rows_out[base + 3 : base + 5] = sums2[0:2]
        rows_out[base + 5 : base + 6] = sums2[3:4]
        rows_out[base + 6 : base + 10] = up_bias_grad[...]
        rows_out[base + 15 : base + 16] = jnp.zeros((1, rows_out.buffer.shape[1]), F32)
        for copy in leaving:
            copy.wait()

    rows = SMALL_ROWS * (len(little) - 1)
    outs = [jax.ShapeDtypeStruct((rows, width), F32), jax.ShapeDtypeStruct((count, width), F32)]
    whole = jax.ShapeDtypeStruct((4, inner, width), BF)
    part = jax.ShapeDtypeStruct((4, inner // 2, width), BF)
    ordered = [normed, incoming, places]
    for grad_query, grad_kept, came_key, came_value, query, kept, cosine, sine, mixed in sides:
        ordered += [mixed, grad_query, query, grad_kept, came_key, came_value, kept, cosine, sine]
    found = staged(
        body, "qkv_back", 32 * count * width * 2 * inner, x_bit,
        ordered + [gain, inputs_kept, grad_middle] + list(little), tuple(near) + tuple(far), outs,
        ([whole] + [part] * 2) * 2,
        (
            pltpu.VMEM((2, 4, 2 * inner, width), BF),
            pltpu.VMEM((2, 4, 2 * inner, width), BF),
            pltpu.SemaphoreType.DMA((6,)),
            pltpu.SemaphoreType.DMA((40,)),
        ),
        gates,
    )
    return (found[2], found[3:5], found[5], found[6:8]), found[:2]


def run_tasks(place, tasks, gates, alone):
    inputs = [item for task in tasks for item in task[0]]
    outs = [jax.ShapeDtypeStruct(*item) for task in tasks for item in task[1]]

    def body(at, sources, _, results, __):
        for task in tasks:
            task[2](at[0], sources[: len(task[0])], results[: len(task[1])])
            sources, results = sources[len(task[0]) :], results[len(task[1]) :]

    if alone:

        def kernel(at, *refs):
            body(at, refs[: len(inputs)], (), refs[len(inputs) + len(gates) :], ())

        found = pl.pallas_call(
            kernel,
            out_shape=outs,
            in_specs=[SCALAR] + [WHOLE] * len(inputs) + [PLACE] * len(gates),
            out_specs=[WHOLE] * len(outs),
            compiler_params=pltpu.CompilerParams(vmem_limit_bytes=24 * 2**20),
            name="sums_alone",
            cost_estimate=pl.CostEstimate(flops=0, bytes_accessed=2**20, transcendentals=0),
        )(place, *inputs, *gates)
    else:
        found = staged(body, "sums", 0, place, inputs, (), outs, gates=gates)
    given = []
    for task in tasks:
        given.append(found[: len(task[1])])
        found = found[len(task[1]) :]
    return given


def wide(ref):
    return ref[...].astype(F32)


class Piece:
    def __init__(self, swapped=False):
        self.swapped = swapped

    def begin(self, found):
        self.own, first, self.second, third = found
        self.came_near = [over_core(item) for item in first]
        self.came_far = [over_core(item) for item in third]
        return self.came_near + self.came_far

    def sources(self):
        return (self.own, self.second, *self.came_near, *self.came_far)

    def sum_of(self, sources, quarter, slot, high):
        mine = sources[quarter]
        many = (len(sources) - 2) // 2
        parts = sources[2 + many * quarter : 2 + many * (quarter + 1)]
        if mine.shape[0] == 2:
            rows = mine.shape[1] // 2
            own = mine[slot, high * rows : (high + 1) * rows]
            came = jnp.concatenate([parts[2 * high][slot], parts[2 * high + 1][slot]], axis=0)
        else:
            own = mine[2 * slot + high]
            came = jnp.concatenate([part[2 * slot + high] for part in parts], axis=0)
        return own.astype(F32) + came.astype(F32)

    def size(self):
        slots, rows, width = self.own.shape
        return slots * rows // 4, width

    def cross(self):
        half, width = self.size()

        def sums(at, sources, results):
            del at
            for slot in range(2):
                results[0][slot] = self.sum_of(sources, 1, slot, 0).astype(BF)
                results[1][slot] = self.sum_of(sources, 0, slot, 0).astype(BF)
                results[2 + slot][0] = self.sum_of(sources, 0, slot, 1).astype(BF)
                results[2 + slot][1] = self.sum_of(sources, 1, slot, 1).astype(BF)

        def after(found):
            up, self.low, self.high, away = found
            self.across, self.sideways = over_y(up), over_bit(away, 0)
            return [self.across, self.sideways]

        return self.sources(), [((2, half, width), BF)] * 4, sums, after

    def turn(self):
        _, half, width = self.low.shape

        def sums(at, sources, results):
            del at
            for way in range(2):
                results[2 * way][...] = sources[2 * way][0].astype(F32) + sources[2 * way + 1][0].astype(F32)
                results[2 * way + 1][...] = (
                    sources[2 * way][1].astype(F32) + sources[2 * way + 1][1].astype(F32)
                ).astype(BF)

        def after(found):
            self.low_kept, low, self.high_kept, high = found
            self.low_came, self.high_came = over_bit(low, 0), over_y(high)
            return [self.low_came, self.high_came]

        shapes = [((half, width), F32), ((half, width), BF)] * 2
        return (self.low, self.across, self.high, self.sideways), shapes, sums, after

    def total_parts(self):
        if self.kept is None:
            inputs = (self.low_kept, self.low_came, self.high_kept, self.high_came)
            rows, width = self.low_kept.shape

            def total(sources):
                low, high = wide(sources[0]) + wide(sources[1]), wide(sources[2]) + wide(sources[3])
                return jnp.concatenate([low, high], axis=0)

            return inputs, 2 * rows, width, total

        def total(sources):
            result = wide(sources[0])
            for source in sources[1:]:
                result = result + wide(source)
            return result

        return (self.kept,) + tuple(self.came), self.kept.shape[0], self.kept.shape[1], total

    def halve(self, bit):
        inputs, rows, width, total_of = self.total_parts()
        half = rows // 2

        def sums(at, sources, results):
            total = total_of(sources)
            low, high = total[:half], total[half:]
            first = ((at >> bit) & 1) == 0
            results[0][...] = jnp.where(first, low, high)
            results[1][...] = jnp.where(first, high, low).astype(BF)

        def after(found):
            self.kept = found[0]
            self.came = (over_bit(found[1], bit),)
            return list(self.came)

        return inputs, [((half, width), F32), ((half, width), BF)], sums, after

    def whole(self):
        inputs, rows, width, total_of = self.total_parts()

        def sums(at, sources, results):
            del at
            results[0][...] = total_of(sources).astype(BF)

        return inputs, [((rows, width), BF)], sums, self.spread

    def spread(self, found):
        self.total = found[0]
        self.others = (over_bit(self.total, self.ways.pop()),)
        return list(self.others)

    def join(self, bit):
        rows, width = self.total.shape

        def sums(at, sources, results):
            first = ((at >> bit) & 1) == 0
            mine, other = sources[0][...], sources[1][...]
            results[0][:rows] = jnp.where(first, mine, other)
            results[0][rows:] = jnp.where(first, other, mine)

        return (self.total,) + self.others, [((2 * rows, width), BF)], sums, self.spread

    def tasks(self):
        bits = lax.axis_size("dp").bit_length() - 1
        self.kept = None
        calls = [self.cross, self.turn] + [partial(self.halve, bit) for bit in range(1, bits)]
        self.ways = list(range(bits))
        if self.swapped and bits > 1:
            self.ways[:2] = [1, 0]
        calls += [self.whole] + [partial(self.join, bit) for bit in reversed(self.ways[1:])]
        return calls

    def result(self, bit):
        return (
            jnp.where(bit == 0, self.total, self.others[0]).astype(F32),
            jnp.where(bit == 0, self.others[0], self.total).astype(F32),
        )


class Whole(Piece):
    def over(self):
        half, width = self.size()

        def sums(at, sources, results):
            del at
            for slot in range(2):
                for high in range(2):
                    rows = slice(high * half, (high + 1) * half)
                    results[0][slot, rows] = self.sum_of(sources, 1, slot, high).astype(BF)
                    results[1][slot, rows] = self.sum_of(sources, 0, slot, high).astype(BF)

        def after(found):
            self.across, self.low = over_y(found[0]), found[1]
            return [self.across]

        return self.sources(), [((2, 2 * half, width), BF)] * 2, sums, after

    def along(self):
        def sums(at, sources, results):
            del at
            results[0][...] = (wide(sources[0]) + wide(sources[1])).astype(BF)

        def after(found):
            self.total = lax.psum(found[0], "dp")
            return []

        return (self.low, self.across), [(self.low.shape, BF)], sums, after

    def tasks(self):
        return [self.over, self.along]

    def result(self, bit):
        del bit
        return self.total[0].astype(F32), self.total[1].astype(F32)


class Small:
    def __init__(self, rows):
        self.mine, self.other = rows, over_core(rows)

    def add(self, quarter_bit, mine, other, result):
        rows, width = mine.shape
        lanes = width // 4
        if not quarter_bit:
            result[...] = mine[...] + other[...]
            return
        for base in range(0, rows, SMALL_ROWS):
            result[base : base + 6] = mine[base : base + 6] + other[base : base + 6]
            for quarter in range(4):
                own, partner = base + 6 + quarter, base + 6 + (quarter ^ quarter_bit)
                result[own : own + 1] = mine[own : own + 1] + other[partner : partner + 1]
            tail = other[base + 8 : base + SMALL_ROWS]
            if quarter_bit == 2:
                moved = pltpu.roll(tail, 2 * lanes, 1)
            else:
                lane = lax.broadcasted_iota(jnp.int32, tail.shape, 1)
                moved = jnp.where(
                    lane % (2 * lanes) < lanes, pltpu.roll(tail, 3 * lanes, 1), pltpu.roll(tail, lanes, 1)
                )
            result[base + 10 : base + SMALL_ROWS] = mine[base + 10 : base + SMALL_ROWS] + moved[2:]

    def step(self, quarter_bit, move):
        rows, width = self.mine.shape

        def sums(at, sources, results):
            del at
            self.add(quarter_bit, *sources, results[0])

        def after(found):
            self.mine = found[0]
            self.other = move(self.mine)
            return [self.other]

        return (self.mine, self.other), [((rows, width), F32)], sums, after

    def last(self):
        rows, width = self.mine.shape
        layers, lanes = rows // SMALL_ROWS, width // 4

        def sums(at, sources, results):
            del at
            self.add(2, *sources, results[9])
            total = results[9][...]
            for layer in range(layers):
                base = SMALL_ROWS * (layers - 1 - layer)
                for item in range(7):
                    results[item][layer : layer + 1] = total[base + item : base + item + 1]
                results[7][layer] = total[base + 10 : base + 13, :lanes]
                turned = total[base + 13 : base + 15, :lanes]
                results[8][layer] = jnp.concatenate(
                    [
                        turned[:, at : at + HALF] + turned[:, at + HALF : at + HEAD_DIM]
                        for at in range(0, lanes, HEAD_DIM)
                    ],
                    axis=1,
                )

        def after(found):
            self.found = found
            return []

        shapes = [((layers, width), F32)] * 7 + [((layers, 3, lanes), F32), ((layers, 2, lanes // 2), F32)]
        shapes.append(((rows, width), F32))
        return (self.mine, self.other), shapes, sums, after

    def tasks(self):
        bits = lax.axis_size("dp").bit_length() - 1
        moves = [partial(over_bit, bit=bit) for bit in (1, 0, *range(2, bits))] + [over_y]
        quarters = [1] + [0] * bits
        return [partial(self.step, *item) for item in zip(quarters, moves)] + [self.last]


def attention_outputs(place, pieces):
    _, width = pieces[0].total.shape
    inner = pieces[0].total.shape[0] // 2
    layers = len(pieces)

    def body(numbers, inputs, _, results, __):
        for layer in reversed(range(layers)):
            mine, other = inputs[2 * layer : 2 * layer + 2]
            ahead = ((numbers[0] >> 1) & 1) == 0
            first = jnp.where(ahead, mine[...], other[...]).astype(F32)
            second = jnp.where(ahead, other[...], mine[...]).astype(F32)
            results[0][layer, 0] = first[:inner]
            results[0][layer, 1] = second[:inner]
            results[0][layer, 2] = first[inner:]
            results[0].leave(layer)
            results[1][layer] = second[inner:]
            results[1].leave(layer)

    items = [item for piece in pieces for item in (piece.total, piece.others[0])]
    return staged(
        body, "attention_outputs", 0, place, items, (),
        (jax.ShapeDtypeStruct((layers, 3, inner, width), F32), jax.ShapeDtypeStruct((layers, inner, width), F32)),
    )


def over_bits(values, mask):
    size = lax.axis_size("dp")
    return lax.ppermute(values, "dp", [(at, at ^ mask) for at in range(size)])


def over_both(values):
    return lax.ppermute(values, "tensor", [(at, at ^ 3) for at in range(4)])


class FarFetch:
    def __init__(self, half):
        self.mine = over_y(half)

    def turn(self, hold):
        self.mine, _ = lax.optimization_barrier((self.mine, hold))
        self.other = over_bit(self.mine, 0)
        self.mine_core = over_core(self.mine)

    def end(self, hold):
        self.other, _ = lax.optimization_barrier((self.other, hold))
        self.found = (self.mine, self.other, self.mine_core, over_core(self.other))


def body(
    tokens,
    out_grad,
    image_lengths,
    norm1_gain,
    norm1_bias,
    qkv_weight,
    qkv_bias,
    rope_freqs,
    out_weight,
    out_bias,
    norm2_gain,
    norm2_bias,
    up_weight,
    up_bias,
    down_weight,
    down_bias,
):
    count, width = tokens.shape
    inner = qkv_weight.shape[3]
    heads = inner // HEAD_DIM
    me = lax.axis_index("tensor")
    xbit = lax.axis_index("dp") & 1
    x_bit = jnp.stack([xbit, xbit]).astype(jnp.int32)
    x_bit_plain = jnp.stack([xbit, jnp.zeros_like(xbit)]).astype(jnp.int32)

    small = jnp.concatenate(
        [qkv_bias.reshape(LAYERS, -1), rope_freqs.reshape(LAYERS, -1), up_bias], axis=1
    )
    near_small, far_small = (small, over_core(small)), (over_y(small), over_both(small))

    lengths = lax.dynamic_index_in_dim(image_lengths, me // 2, 0, keepdims=False)
    half_at = me % 2
    position = jnp.arange(count, dtype=jnp.int32)
    segment, row_at, column_at = places_at(lengths, position + half_at * count)
    segment_other, _, _ = places_at(lengths, position + (1 - half_at) * count)
    here_segment = segment[:, None].astype(F32)
    all_segments = jnp.concatenate([segment, segment_other])[None, :].astype(F32)
    places = jnp.stack([row_at, column_at], axis=1).astype(F32)

    qkv_turned = jnp.swapaxes(qkv_weight, 2, 3)
    near_att, far_att, near_mlp, far_mlp = [], [], [], []

    def fetch_att(layer, gates=()):
        packed, half = pack(layer, x_bit, qkv_turned, out_weight[:, None], 2, gates)
        near_att.append((packed, over_core(packed)))
        far_att.append(FarFetch(half))

    def fetch_mlp(layer, gates=()):
        both, half = pack(layer, x_bit, up_weight[:, None], down_weight[:, None], 1, gates)
        near_mlp.append((both, over_core(both)))
        far_mlp.append(FarFetch(half[0]))

    current = tokens
    kept_layers = []
    cosines, sines = [[] for _ in range(LAYERS)], [[] for _ in range(LAYERS)]
    before = ()
    fetch_att(0)
    for l in range(LAYERS):
        inputs = current
        gain, shift = norm1_gain[l : l + 1], norm1_bias[l : l + 1]
        queries, keeps, comes, mixes, spreads, exps = [], [], [], [], [], []

        def project(side, source, weights):
            nonlocal before
            found = qkv_part(
                side == 0, l, x_bit, source, gain, shift, (near_small, far_small)[side], places, weights, before
            )
            before = (found[0],)
            queries.append(found[0])
            keeps.append(found[1])
            comes.append(over_core(found[2]))
            cosines[l].append(found[3])
            sines[l].append(found[4])
            return found

        def mix(side):
            nonlocal before
            found = attend(queries[side], keeps[side], comes[side], here_segment, all_segments, x_bit, before)
            before = (found[0],)
            mixes.append(found[0])
            spreads.append(found[1])
            exps.append(found[2])

        normed = project(0, inputs, near_att[l])[5]
        if l:
            far_mlp[l].turn(queries[0])
        if l == 0:
            fetch_mlp(0, before + far_small)
            before = (near_mlp[0][0],)
            far_att[0].turn(near_mlp[0][0])
            mix(0)
            fetch_att(1, before)
            before = (near_att[1][0],)
            far_att[0].end(mixes[0])
            far_mlp[0].turn(mixes[0])
            project(1, normed, far_att[0].found)
            mix(1)
            fetch_mlp(1, before)
            before = (near_mlp[1][0],)
            far_att[1].turn(mixes[1])
            far_mlp[0].end(mixes[1])
        else:
            project(1, normed, far_att[l].found)
            mix(0)
            mix(1)
            far_mlp[l].end(mixes[1])
        middle, normed_mlp, active_near, slope_near, total = mlp_near(
            l, x_bit, inputs, mixes[0], mixes[1], out_bias[l : l + 1], norm2_gain[l : l + 1], norm2_bias[l : l + 1],
            near_small, down_bias[l : l + 1], near_att[l] + far_att[l].found, near_mlp[l], before,
        )
        active_far, slope_far, current = mlp_far(
            l, x_bit, normed_mlp, total, far_small, far_mlp[l].found, BF if l == LAYERS - 1 else F32
        )
        before = (current,)
        if l == 0:
            far_att[1].end(middle)
        kept_layers.append(
            (inputs, normed, queries, keeps, comes, mixes, spreads, exps, middle, normed_mlp, (active_near, active_far), (slope_near, slope_far))
        )
    activations = current

    gradient = out_grad
    small_rows = []
    summed = [None] * LAYERS
    waiting = []
    todo = []
    clock = 0
    latest = []
    here = lax.axis_index("dp").reshape(1).astype(jnp.int32)

    def ran(found):
        latest[:] = found[:1]
        return found

    def wait_until(arrays, when):
        waiting.append((when, arrays))

    def gates_now():
        nonlocal clock
        clock += 1
        due = [array for when, arrays in waiting if when <= clock for array in arrays]
        waiting[:] = [item for item in waiting if item[0] > clock]
        turn = [entry for entry in todo if entry[0] == clock]
        todo[:] = [entry for entry in todo if entry[0] != clock]
        if not turn:
            return due + latest
        tasks = [step() for _, _, step in turn]
        found = run_tasks(here, [task[:3] for task in tasks], due + latest, clock > 3 * LAYERS + 1)
        for (_, length, _), task, given in zip(turn, tasks, found):
            wait_until(task[3](given), clock + length)
        latest[:] = found[0][:1]
        return latest

    def plan(piece, base, table):
        start, length = 0, 1
        for at, step in enumerate(piece.tasks()):
            start, length = table[at] if at < len(table) else (start + length, 1)
            todo.append((base + start, length, step))

    for l in reversed(range(LAYERS)):
        (inputs, normed, queries, keeps, comes, mixes, spreads, exps, middle, normed_mlp, active, slope) = kept_layers[l]
        att = (near_att[l], far_att[l].found)
        pieces = [Piece(), Piece(swapped=True)]
        tables = PLANS[l > 0]
        for piece, table in zip(pieces, tables):
            plan(piece, clock, table)
        found, rest = mlp_back(
            x_bit, gradient, normed_mlp, middle, norm2_gain[l : l + 1], active, slope, near_mlp[l],
            far_mlp[l].found, gates_now(),
        )
        ran(rest)
        up_bias_grad, sums2, grad_middle, incoming = rest
        wait_until(pieces[0].begin(found), clock + tables[0][0][0] - 1)
        backs = attend_back(
            x_bit, incoming,
            [(queries[side], keeps[side], comes[side], mixes[side], spreads[side], exps[side]) for side in range(2)],
            *att, gates_now(),
        )
        ran(backs[0])
        sides = [
            (back[0], back[1], over_core(back[2]), over_core(back[3]), queries[side], keeps[side], cosines[l][side], sines[l][side], mixes[side])
            for side, back in enumerate(backs)
        ]
        found, rest = qkv_back(
            x_bit, normed, incoming, places, sides, *att, norm1_gain[l : l + 1], inputs, grad_middle,
            [sums2, up_bias_grad] + small_rows, gates_now(),
        )
        ran(rest)
        rows, gradient = rest
        small_rows = [rows]
        wait_until(pieces[1].begin(found), clock + tables[1][0][0] - 3)
        summed[l] = pieces

    little = Small(small_rows[0])
    wait_until([little.other], clock + SMALL_PLAN[0][0])
    plan(little, clock, SMALL_PLAN)
    while todo:
        gates_now()
    gain1, shift1, bias_out, gain2, shift2, bias_down, bias_up, bias_qkv, turns = little.found[:9]
    grad_qkv, grad_out = attention_outputs(here, [summed[l][1] for l in range(LAYERS)])
    grad_up, grad_down = zip(*(summed[l][0].result(xbit) for l in range(LAYERS)))
    return (
        activations,
        gradient,
        gain1,
        shift1,
        jnp.swapaxes(grad_qkv, 2, 3),
        bias_qkv,
        turns,
        grad_out,
        bias_out,
        gain2,
        shift2,
        jnp.stack(grad_up),
        bias_up,
        jnp.stack(grad_down),
        bias_down,
    )


def solution(mesh):
    in_specs = (
        P(("dp", "tensor"), None),
        P(("dp", "tensor"), None),
        P("dp", None),
        P(),
        P(),
        P(None, None, None, "tensor"),
        P(None, None, "tensor"),
        P(None, None, "tensor"),
        P(None, "tensor", None),
        P(),
        P(),
        P(),
        P(None, None, "tensor"),
        P(None, "tensor"),
        P(None, "tensor", None),
        P(),
    )
    out_specs = (
        P(("dp", "tensor"), None),
        P(("dp", "tensor"), None),
        P(),
        P(),
        P(None, None, None, "tensor"),
        P(None, None, "tensor"),
        P(None, None, "tensor"),
        P(None, "tensor", None),
        P(),
        P(),
        P(),
        P(None, None, "tensor"),
        P(None, "tensor"),
        P(None, "tensor", None),
        P(),
    )
    return jax.shard_map(body, mesh=mesh, in_specs=in_specs, out_specs=out_specs, check_vma=False)
```

```python
from functools import partial

import jax
import jax.numpy as jnp
from jax import lax
from jax.experimental import pallas as pl
from jax.experimental.pallas import tpu as pltpu
from jax.sharding import PartitionSpec as P

HEAD_DIM = 64
LEN = 832
SIDE_S = 14
SIDE_M = 20
SIDE_L = 24
MAX_IMAGES = 4
LAYERS = 2

EPS = 1e-06
NEGATIVE = -1000000000.0
BF = jnp.bfloat16
F32 = jnp.float32

CORE = [(0, 1), (1, 0), (2, 3), (3, 2)]
ACROSS = [(0, 2), (2, 0), (1, 3), (3, 1)]


def over_core(values):
    return lax.ppermute(values, "tensor", CORE)


def over_y(values):
    return lax.ppermute(values, "tensor", ACROSS)


def over_bit(values, bit):
    size = lax.axis_size("dp")
    return lax.ppermute(values, "dp", [(at, at ^ (1 << bit)) for at in range(size)])


def places_at(lengths, position):
    ends = jnp.cumsum(lengths)
    starts = ends - lengths
    segment = jnp.sum((position[:, None] >= ends[None, :]).astype(jnp.int32), axis=1)
    belongs = segment[:, None] == jnp.arange(MAX_IMAGES, dtype=jnp.int32)[None, :]
    begin_at = jnp.sum(jnp.where(belongs, starts[None, :], 0), axis=1)
    size = jnp.sum(jnp.where(belongs, lengths[None, :], 0), axis=1)
    side = jnp.where(
        size == SIDE_S * SIDE_S, SIDE_S, jnp.where(size == SIDE_M * SIDE_M, SIDE_M, SIDE_L)
    ).astype(jnp.int32)
    offset = position - begin_at
    inside = segment < MAX_IMAGES
    row_at = jnp.where(inside, offset // side, 0)
    column_at = jnp.where(inside, offset % side, 0)
    return segment, row_at, column_at


PLANS = (
    (
        ((3, 2), (5, 1), (6, 1), (7, 1), (8, 1), (9, 1), (10, 9)),
        ((4, 1), (5, 1), (6, 1), (7, 1), (8, 1), (9, 1), (10, 9)),
    ),
    (
        ((3, 1), (4, 1), (5, 1), (6, 1), (7, 1), (8, 1), (9, 1)),
        ((5, 1), (6, 1), (7, 1), (8, 1), (9, 1), (10, 1), (13, 1)),
    ),
)
SMALL_PLAN = ((3, 1), (4, 1), (5, 1), (6, 1), (7, 1))
VMEM_BYTES = 58 * 2**20
PARAMS = pltpu.CompilerParams(vmem_limit_bytes=VMEM_BYTES)
WHOLE = pl.BlockSpec(memory_space=pltpu.VMEM)
PLACE = pl.BlockSpec(memory_space=pl.ANY)
SCALAR = pl.BlockSpec(memory_space=pltpu.SMEM)
HALF = HEAD_DIM // 2
SIDE_ROWS = 32
SMALL_ROWS = 16


def dot(left, right, on_left, on_right):
    return lax.dot_general(
        left, right, (((on_left,), (on_right,)), ((), ())), preferred_element_type=F32
    )


def norm_parts(values):
    average = jnp.mean(values, axis=-1, keepdims=True)
    centred = values - average
    variance = jnp.mean(centred * centred, axis=-1, keepdims=True)
    inverse = lax.rsqrt(variance + EPS)
    return centred * inverse, inverse


def norm_back(values, gain, incoming):
    xhat, inverse = norm_parts(values)
    grad_gain = jnp.sum(incoming * xhat, axis=0, keepdims=True)
    grad_shift = jnp.sum(incoming, axis=0, keepdims=True)
    scaled = incoming * gain
    through = inverse * (
        scaled
        - jnp.mean(scaled, axis=-1, keepdims=True)
        - xhat * jnp.mean(scaled * xhat, axis=-1, keepdims=True)
    )
    return through, grad_gain, grad_shift


def first_half(shape):
    return lax.broadcasted_iota(jnp.int32, shape, 1) % HEAD_DIM < HALF


def swap(values):
    width = values.shape[1]
    return jnp.where(
        first_half(values.shape),
        pltpu.roll(values, width - HALF, 1),
        pltpu.roll(values, HALF, 1),
    )


def one_head(values, head):
    lane = lax.broadcasted_iota(jnp.int32, values.shape, 1)
    return jnp.where((lane < HEAD_DIM) == (head == 0), values, jnp.zeros_like(values))


def join_heads(first, second):
    lane = lax.broadcasted_iota(jnp.int32, first.shape, 1)
    return jnp.where(lane < HEAD_DIM, first, second)


class Held:
    def __init__(self, source, buffer, sem):
        self.copy, self.buffer, self.done = pltpu.make_async_copy(source, buffer, sem), buffer, False
        self.shape, self.dtype = buffer.shape, buffer.dtype
        self.copy.start()

    def wait(self):
        if not self.done:
            self.copy.wait()
            self.done = True

    def __getitem__(self, at):
        self.wait()
        return self.buffer[at]


class Given:
    def __init__(self, target, buffer, sems):
        self.target, self.buffer, self.sems, self.copies = target, buffer, sems, []

    def __setitem__(self, at, values):
        self.buffer[at] = values

    def __getitem__(self, at):
        return self.buffer[at]

    def leave(self, at=None):
        source, target = self.buffer, self.target
        if at is not None:
            source, target = source.at[at], target.at[at]
        self.copies.append(pltpu.make_async_copy(source, target, self.sems.at[len(self.copies)]))
        self.copies[-1].start()


PIECES_OUT = 6


def staged(body, name, flops, scalars, inputs, raws, outs, raw_outs=(), scratch=(), gates=()):
    counts = [len(inputs), len(raws), len(gates), len(outs), len(raw_outs)]

    def kernel(numbers, *refs):
        groups = []
        for count in counts:
            groups.append(refs[:count])
            refs = refs[count:]
        sources, plain, _, targets, plain_targets = groups
        in_buffers, out_buffers, rest = refs[: counts[0]], refs[counts[0] : counts[0] + counts[3]], refs[counts[0] + counts[3] :]
        in_sems, out_sems, rest = rest[0], rest[1], rest[2:]
        held = [Held(*item, in_sems.at[at]) for at, item in enumerate(zip(sources, in_buffers))]
        given = [Given(*item, out_sems.at[at]) for at, item in enumerate(zip(targets, out_buffers))]
        body(numbers, held, plain, given, plain_targets, *rest)
        for item in held:
            item.wait()
        for item in given:
            if not item.copies:
                item.leave()
        for item in given:
            for copy in item.copies:
                copy.wait()

    return pl.pallas_call(
        kernel,
        out_shape=list(outs) + list(raw_outs),
        in_specs=[SCALAR] + [PLACE] * sum(counts[:3]),
        out_specs=[PLACE] * sum(counts[3:]),
        scratch_shapes=[pltpu.VMEM(item.shape, item.dtype) for item in list(inputs) + list(outs)]
        + [pltpu.SemaphoreType.DMA((max(counts[0], 1),)), pltpu.SemaphoreType.DMA((max(counts[3], 1), PIECES_OUT))]
        + list(scratch),
        compiler_params=PARAMS,
        name=name,
        cost_estimate=pl.CostEstimate(flops=flops // 8, bytes_accessed=2**20, transcendentals=0),
    )(scalars, *inputs, *raws, *gates)


def fetch(pairs, sems):
    copies = [pltpu.make_async_copy(source, target, sems.at[at]) for at, (source, target) in enumerate(pairs)]
    for copy in copies:
        copy.start()
    return copies


def att_pairs(near, refs, into, xbit, parts):
    inner = into.shape[1] // 2
    low, high = pl.ds(0, inner), pl.ds(inner, inner)
    if near:
        return [(refs[0].at[pl.ds(0, parts)], into.at[pl.ds(0, parts), low]), (refs[1].at[pl.ds(0, parts)], into.at[pl.ds(0, parts), high])]
    mine, other = pl.ds(2 * xbit, 2), pl.ds(2 - 2 * xbit, 2)
    return [
        (refs[0], into.at[mine, low]),
        (refs[1], into.at[other, low]),
        (refs[2], into.at[mine, high]),
        (refs[3], into.at[other, high]),
    ]


def mlp_pairs(near, refs, into, xbit):
    if near:
        return [(ref, into.at[quarter]) for quarter, ref in enumerate(refs)]
    slots = ((0, xbit), (0, 1 - xbit), (1, xbit), (1, 1 - xbit))
    return [(ref, into.at[quarter, slot]) for ref, (quarter, slot) in zip(refs, slots)]


def pack(layer, x_bit, first, second, cut, gates=()):
    _, rows, width, inner = first.shape
    more = second.shape[1]

    def body(numbers, _, raws, __, targets, held, sems):
        whole, half = targets
        for copy in fetch(
            [(raws[0].at[layer], held.at[pl.ds(0, rows)]), (raws[1].at[layer], held.at[pl.ds(rows, more)])], sems
        ):
            copy.wait()
        copies = [
            pltpu.make_async_copy(held.at[pl.ds(cut * numbers[0], cut)], half, sems.at[2]),
            pltpu.make_async_copy(held, whole, sems.at[3]),
        ]
        for copy in copies:
            copy.start()
        for copy in copies:
            copy.wait()

    return staged(
        body, "pack", 0, x_bit, (), (first, second), (),
        (
            jax.ShapeDtypeStruct((rows + more, width, inner), BF),
            jax.ShapeDtypeStruct((cut, width, inner), BF),
        ),
        (pltpu.VMEM((rows + more, width, inner), BF), pltpu.SemaphoreType.DMA((4,))), gates,
    )


def angle_tables(freqs, places):
    steps = lax.broadcasted_iota(jnp.int32, (SIDE_ROWS, 1), 0).astype(F32)
    found = []
    for axis in range(2):
        terms = steps * freqs[axis]
        table = jnp.concatenate([jnp.cos(terms), jnp.sin(terms)], axis=1)
        at = places[:, axis : axis + 1]
        column = lax.broadcasted_iota(jnp.int32, (places.shape[0], SIDE_ROWS), 1).astype(F32)
        chosen = lax.dot_general(
            (column == at).astype(F32), table, (((1,), (0,)), ((), ())),
            precision=lax.Precision.HIGHEST, preferred_element_type=F32,
        )
        width = terms.shape[1]
        found.append((chosen[:, :width], chosen[:, width:]))
    (row_cos, row_sin), (col_cos, col_sin) = found
    cosine = row_cos * col_cos - row_sin * col_sin
    sine = row_sin * col_cos + row_cos * col_sin
    return cosine, jnp.where(first_half(sine.shape), -sine, sine)


def qkv_part(near, layer, x_bit, source, gain, shift, small, places, weights, gates=()):
    count, width = source.shape
    inner = weights[0].shape[1]

    def body(numbers, inputs, raws, results, _, held, sems):
        gain, shift, places, first, second, source = inputs
        query, kept, sent, cosine, sine = results[:5]
        copies = fetch(att_pairs(near, raws, held, numbers[0], 3), sems)
        both = [item[layer : layer + 1] for item in (first, second)]
        bias = [
            jnp.concatenate([item[:, part * inner : (part + 1) * inner] for item in both], axis=1)
            for part in range(3)
        ]
        freqs = []
        for axis in range(2):
            begin = 3 * inner + axis * (inner // 2)
            pieces = [item[:, at : at + HALF] for item in both for at in range(begin, begin + inner // 2, HALF)]
            freqs.append(jnp.concatenate([piece for piece in pieces for _ in range(2)], axis=1))
        cosine[...], sine[...] = angle_tables(freqs, places[...])
        cosine.leave()
        sine.leave()
        if near:
            xhat, _ = norm_parts(source[...].astype(F32))
            normed = (xhat * gain[...] + shift[...]).astype(BF)
            results[5][...] = normed
            results[5].leave()
        else:
            normed = source[...]
        for copy in copies:
            copy.wait()
        for part in (1, 2, 0):
            values = dot(normed, held[part], 1, 1) + bias[part]
            if part < 2:
                values = values * cosine[...] + swap(values) * sine[...]
            if part == 0:
                query[...] = (values * HEAD_DIM**-0.5).astype(BF)
            else:
                kept[part - 1] = values.astype(BF)
                sent[part - 1] = pltpu.roll(values, inner, 1).astype(BF)
                sent.leave(part - 1)

    pair = jax.ShapeDtypeStruct((2, count, 2 * inner), BF)
    table = jax.ShapeDtypeStruct((count, 2 * inner), F32)
    outs = [jax.ShapeDtypeStruct((count, 2 * inner), BF), pair, pair, table, table]
    if near:
        outs.append(jax.ShapeDtypeStruct((count, width), BF))
    return staged(
        body, "qkv_near" if near else "qkv_far", 2 * count * width * 6 * inner, x_bit,
        (gain, shift, places, *small, source), weights, outs,
        scratch=(pltpu.VMEM((4, 2 * inner, width), BF), pltpu.SemaphoreType.DMA((len(weights),))), gates=gates,
    )


def attend(query, kept, came, here, there, number, gates=()):
    count, width = query.shape
    heads = width // HEAD_DIM

    def body(_, inputs, __, results, ___):
        query, kept, here, came, there = inputs
        mixed, spread, exps = results
        allowed = here[...] == there[...]
        for pair in range(heads // 2):
            lanes = slice(2 * HEAD_DIM * pair, 2 * HEAD_DIM * (pair + 1))
            keys = jnp.concatenate([kept[0, :, lanes], came[0, :, lanes]], axis=0)
            values = jnp.concatenate([kept[1, :, lanes], came[1, :, lanes]], axis=0)
            outs, inverses = [], []
            for head in range(2):
                scores = dot(one_head(query[:, lanes], head), keys, 1, 1)
                scores = jnp.where(allowed, scores, NEGATIVE)
                highest = jnp.max(scores, axis=1, keepdims=True)
                raised = jnp.exp(scores - highest)
                inverse = 1.0 / jnp.sum(raised, axis=1, keepdims=True)
                low = raised.astype(BF)
                exps[2 * pair + head] = low
                exps.leave(2 * pair + head)
                outs.append(dot(low, values, 1, 0) * inverse)
                inverses.append(jnp.broadcast_to(inverse, outs[0].shape))
            mixed[:, lanes] = join_heads(*outs).astype(BF)
            spread[:, lanes] = join_heads(*inverses)

    return staged(
        body, "attend", 8 * count * width * 768, number, (query, kept, here, came, there), (),
        (
            jax.ShapeDtypeStruct((count, width), BF),
            jax.ShapeDtypeStruct((count, width), F32),
            jax.ShapeDtypeStruct((heads, count, 2 * count), BF),
        ),
        gates=gates,
    )


def gelu_parts(pre):
    size = jnp.abs(pre)
    ratio = 1.0 / (1.0 + 0.3275911 * (0.5**0.5) * size)
    bell = jnp.exp(-0.5 * pre * pre)
    poly = ((((0.5 * 1.061405429 * ratio - 0.5 * 1.453152027) * ratio + 0.5 * 1.421413741) * ratio - 0.5 * 0.284496736) * ratio + 0.5 * 0.254829592) * ratio
    below = poly * bell
    normal = jnp.where(pre < 0, below, 1.0 - below)
    return pre * normal, normal + pre * (bell * 0.3989422804014327)


def feed(quarter, normed, held, up_bias, active, slope):
    value, rate = gelu_parts(dot(normed, held[quarter, 0], 1, 0) + up_bias[quarter])
    low = value.astype(BF)
    active[quarter] = low
    active.leave(quarter)
    slope[quarter] = rate.astype(BF)
    slope.leave(quarter)
    return dot(low, held[quarter, 1], 1, 0)


def mlp_near(layer, x_bit, inputs, mixed_near, mixed_far, out_bias, gain, shift, small, down_bias, outs, weights, gates=()):
    count, width = inputs.shape
    hidden = weights[0].shape[2]
    inner = outs[0].shape[1]

    def body(numbers, held_inputs, raws, results, _, held_out, held, sems):
        mixed_near, mixed_far, inputs, out_bias, gain, shift, first, second, down_bias = held_inputs
        up_bias = [item[layer : layer + 1, width:] for item in (first, second)]
        middle, normed_out, active, slope, total = results
        xbit = numbers[0]
        copies = fetch(
            [
                (raws[0].at[3], held_out.at[0]),
                (raws[1].at[3], held_out.at[1]),
                (raws[2].at[1], held_out.at[2 + 2 * (1 - xbit)]),
                (raws[3].at[1], held_out.at[2 + 2 * xbit]),
                (raws[4].at[1], held_out.at[3 + 2 * (1 - xbit)]),
                (raws[5].at[1], held_out.at[3 + 2 * xbit]),
            ]
            + mlp_pairs(True, raws[6:], held, xbit),
            sems,
        )
        for copy in copies[:6]:
            copy.wait()
        centre = dot(mixed_near[...], jnp.concatenate([held_out[0], held_out[1]], axis=0), 1, 0)
        centre = centre + dot(mixed_far[...], jnp.concatenate([held_out[2], held_out[3]], axis=0), 1, 0)
        centre = centre + inputs[...].astype(F32) + out_bias[...]
        middle[...] = centre
        middle.leave()
        xhat, _ = norm_parts(centre)
        normed = (xhat * gain[...] + shift[...]).astype(BF)
        normed_out[...] = normed
        normed_out.leave()
        gathered = centre + down_bias[...]
        for quarter in range(2):
            copies[6 + quarter].wait()
            gathered = gathered + feed(quarter, normed, held, up_bias, active, slope)
        total[...] = gathered

    kept = jax.ShapeDtypeStruct((2, count, hidden), BF)
    full = jax.ShapeDtypeStruct((count, width), F32)
    return staged(
        body, "mlp_near", 10 * count * width * width, x_bit,
        (mixed_near, mixed_far, inputs, out_bias, gain, shift, *small, down_bias), tuple(outs) + tuple(weights),
        (full, jax.ShapeDtypeStruct((count, width), BF), kept, kept, full),
        scratch=(
            pltpu.VMEM((6, inner, width), BF),
            pltpu.VMEM((2, 2, width, hidden), BF),
            pltpu.SemaphoreType.DMA((8,)),
        ),
        gates=gates,
    )


def mlp_far(layer, x_bit, normed, total, small, weights, dtype, gates=()):
    count, width = normed.shape
    hidden = weights[0].shape[1]

    def body(numbers, inputs, raws, results, _, held, sems):
        normed, first, second, total = inputs
        up_bias = [item[layer : layer + 1, width:] for item in (first, second)]
        active, slope, result = results
        copies = fetch(mlp_pairs(False, raws, held, numbers[0]), sems)
        gathered = None
        for quarter in range(2):
            for copy in copies[2 * quarter : 2 * quarter + 2]:
                copy.wait()
            term = feed(quarter, normed[...], held, up_bias, active, slope)
            gathered = total[...] + term if gathered is None else gathered + term
        result[...] = gathered.astype(dtype)

    kept = jax.ShapeDtypeStruct((2, count, hidden), BF)
    return staged(
        body, "mlp_far", 8 * count * width * width, x_bit, (normed, *small, total), weights,
        (kept, kept, jax.ShapeDtypeStruct((count, width), dtype)),
        scratch=(pltpu.VMEM((2, 2, width, hidden), BF), pltpu.SemaphoreType.DMA((4,))), gates=gates,
    )


def mlp_back(x_bit, gradient, normed, middle, gain, active, slope, near, far, gates=()):
    count, width = normed.shape
    hidden = active[0].shape[2]

    def body(numbers, inputs, raws, results, grads, held, ready, sems, out_sems):
        gradient, active_far, slope_far, normed, active_near, slope_near, gain, middle = inputs
        bias_grad, sums, grad_middle, low_middle = results
        xbit, up_slot = numbers[0], numbers[1]
        targets = (grads[0:1], grads[1:5], grads[5:6], grads[6:10])
        copies = fetch(
            mlp_pairs(False, raws[2:], held.at[pl.ds(2, 2)], xbit) + mlp_pairs(True, raws[:2], held.at[pl.ds(0, 2)], xbit), sems
        )
        needed = ((copies[4],), (copies[5],), copies[0:2], copies[2:4])
        leaving = []

        def leave(quarter, kind, slot, values):
            ready[quarter, kind] = values.astype(BF)
            rows = targets[quarter][0].shape[1]
            for at, target in enumerate(targets[quarter]):
                copy = pltpu.make_async_copy(
                    ready.at[quarter, kind, pl.ds(at * rows, rows)], target.at[slot], out_sems.at[len(leaving)]
                )
                copy.start()
                leaving.append(copy)

        incoming = gradient[...].astype(F32)
        low = incoming.astype(BF)
        gathered = None
        for quarter in (3, 2, 1, 0):
            active, slope = (active_near, slope_near) if quarter < 2 else (active_far, slope_far)
            leave(quarter, 0, 1 - up_slot, dot(active[quarter % 2], low, 0, 0))
            for copy in needed[quarter]:
                copy.wait()
            inside = dot(low, held[quarter, 1], 1, 1) * slope[quarter % 2].astype(F32)
            low_inside = inside.astype(BF)
            bias_grad[quarter : quarter + 1] = jnp.sum(low_inside.astype(F32), axis=0, keepdims=True)
            leave(quarter, 1, up_slot, dot(normed[...], low_inside, 0, 0))
            term = dot(low_inside, held[quarter, 0], 1, 1)
            gathered = term if gathered is None else gathered + term
        through, grad_gain, grad_shift = norm_back(middle[...], gain[...], gathered)
        result = incoming + through
        grad_middle[...] = result
        grad_middle.leave()
        low_result = result.astype(BF)
        low_middle[...] = low_result
        low_middle.leave()
        sums[0:1] = grad_gain
        sums[1:2] = grad_shift
        sums[2:3] = jnp.sum(low_result.astype(F32), axis=0, keepdims=True)
        sums[3:4] = jnp.sum(low.astype(F32), axis=0, keepdims=True)
        for copy in leaving:
            copy.wait()

    whole = jax.ShapeDtypeStruct((2, width, hidden), BF)
    part = jax.ShapeDtypeStruct((2, width // 4, hidden), BF)
    outs = [
        jax.ShapeDtypeStruct((4, hidden), F32),
        jax.ShapeDtypeStruct((4, width), F32),
        jax.ShapeDtypeStruct((count, width), F32),
        jax.ShapeDtypeStruct((count, width), BF),
    ]
    found = staged(
        body, "mlp_back", 32 * count * width * width, x_bit,
        (gradient, active[1], slope[1], normed, active[0], slope[0], gain, middle), tuple(near) + tuple(far), outs,
        ([whole] + [part] * 4) * 2,
        (
            pltpu.VMEM((4, 2, width, hidden), BF),
            pltpu.VMEM((4, 2, width, hidden), BF),
            pltpu.SemaphoreType.DMA((6,)),
            pltpu.SemaphoreType.DMA((20,)),
        ),
        gates,
    )
    return (found[4], found[5:9], found[9], found[10:14]), found[:4]


def attend_back(x_bit, incoming, sides, near, far, gates=()):
    count, width = sides[0][0].shape
    pairs = width // (2 * HEAD_DIM)
    inner, full = near[0].shape[1:]

    def body(numbers, inputs, raws, results, _, held, sems):
        incoming, xbit = inputs[0], numbers[0]
        copies = fetch(
            [
                (raws[0].at[3], held.at[0]),
                (raws[1].at[3], held.at[1]),
                (raws[2].at[1], held.at[2 + 2 * (1 - xbit)]),
                (raws[3].at[1], held.at[2 + 2 * xbit]),
                (raws[4].at[1], held.at[3 + 2 * (1 - xbit)]),
                (raws[5].at[1], held.at[3 + 2 * xbit]),
            ],
            sems,
        )
        for copy in copies:
            copy.wait()
        for side in (0, 1):
            mixed, spread, kept, came, query, exps = inputs[1 + 6 * side : 7 + 6 * side]
            grad_query, grad_kept, *grad_sent = results[4 * side : 4 * side + 4]
            both = jnp.concatenate([held[2 * side], held[2 * side + 1]], axis=0)
            scaled = dot(incoming[...], both, 1, 1) * spread[...]
            product_all = scaled * mixed[...].astype(F32)
            low_all = scaled.astype(BF)
            for pair in range(pairs):
                lanes = slice(2 * HEAD_DIM * pair, 2 * HEAD_DIM * (pair + 1))
                keys = jnp.concatenate([kept[0, :, lanes], came[0, :, lanes]], axis=0)
                values = jnp.concatenate([kept[1, :, lanes], came[1, :, lanes]], axis=0)
                low_mixed, product = low_all[:, lanes], product_all[:, lanes]
                for_query, for_key, for_value = [], [], []
                for head in range(2):
                    raised = exps[2 * pair + head]
                    level = jnp.sum(one_head(product, head), axis=1, keepdims=True)
                    grad_probs = dot(one_head(low_mixed, head), values, 1, 1)
                    grad_scores = (raised.astype(F32) * (grad_probs - level)).astype(BF)
                    for_value.append(dot(raised, low_mixed, 0, 0))
                    for_query.append(dot(grad_scores, keys, 1, 0))
                    for_key.append(dot(grad_scores, query[:, lanes], 0, 0))
                grad_query[:, lanes] = join_heads(*for_query).astype(BF)
                for part, both_heads in enumerate((for_key, for_value)):
                    joined = join_heads(*both_heads).astype(BF)
                    grad_kept[part, :, lanes] = joined[:count]
                    grad_sent[part][:, lanes] = joined[count:]
            for item in results[4 * side : 4 * side + 4]:
                item.leave()

    shapes = [
        jax.ShapeDtypeStruct((count, width), BF),
        jax.ShapeDtypeStruct((2, count, width), BF),
        jax.ShapeDtypeStruct((count, width), BF),
        jax.ShapeDtypeStruct((count, width), BF),
    ]
    ordered = [incoming]
    for query, kept, came, mixed, spread, exps in sides:
        ordered += [mixed, spread, kept, came, query, exps]
    found = staged(
        body, "attend_back", 32 * count * width * full, x_bit, ordered, tuple(near) + tuple(far), shapes * 2,
        scratch=(pltpu.VMEM((6, inner, full), BF), pltpu.SemaphoreType.DMA((6,))),
        gates=gates,
    )
    return found[:4], found[4:]


def qkv_back(x_bit, normed, incoming, places, sides, near, far, gain, inputs_kept, grad_middle, little, gates=()):
    count, width = normed.shape
    inner = near[0].shape[1]

    def body(numbers, inputs, raws, results, grads, held, ready, sems, out_sems):
        normed, incoming, places = inputs[:3]
        gain, inputs_kept, grad_middle, sums2, up_bias_grad = inputs[21:26]
        rows_out, result = results
        earlier = inputs[26:]
        base = SMALL_ROWS * len(earlier)
        for at, item in enumerate(earlier):
            rows_out[SMALL_ROWS * at : SMALL_ROWS * (at + 1)] = item[...]
        xbit = numbers[0]
        targets = (grads[0:1], grads[1:3], grads[3:4], grads[4:6])
        copies = fetch(
            att_pairs(False, raws[2:], held.at[1], xbit, 3) + att_pairs(True, raws[:2], held.at[0], xbit, 3), sems
        )
        needed = (copies[4:], copies[:4])
        slots = (2 * xbit, 2 * xbit + 1, 2 - 2 * xbit, 3 - 2 * xbit)
        leaving = []

        def store(side, part, values):
            ready[side, part] = values.astype(BF)
            for quarter in range(2):
                rows = targets[2 * side + quarter][0].shape[1]
                for at, target in enumerate(targets[2 * side + quarter]):
                    copy = pltpu.make_async_copy(
                        ready.at[side, part, pl.ds(quarter * inner + at * rows, rows)],
                        target.at[slots[part]],
                        out_sems.at[len(leaving)],
                    )
                    copy.start()
                    leaving.append(copy)

        gathered = None
        for side in (1, 0):
            mixed, grad_query, query, grad_kept, came_key, came_value, kept, cosine, sine = inputs[3 + 9 * side : 12 + 9 * side]
            lanes = slice(2 * inner * side, 2 * inner * (side + 1))
            store(side, 3, dot(mixed[...], incoming[...], 0, 0))
            sign = jnp.where(first_half(query.shape), -1.0, 1.0)
            raw_query = grad_query[...].astype(F32)
            raw_key = grad_kept[0].astype(F32) + pltpu.roll(came_key[...].astype(F32), inner, 1)
            raw_value = grad_kept[1].astype(F32) + pltpu.roll(came_value[...].astype(F32), inner, 1)
            angle = (raw_query * swap(query[...].astype(F32)) + raw_key * swap(kept[0].astype(F32))) * sign
            for axis in range(2):
                rows_out[base + 13 + axis : base + 14 + axis, lanes] = jnp.sum(
                    angle * places[:, axis : axis + 1], axis=0, keepdims=True
                )
            cos, sin = cosine[...], sine[...]
            turned = (
                (raw_query * cos - swap(raw_query) * sin) * HEAD_DIM**-0.5,
                raw_key * cos - swap(raw_key) * sin,
                raw_value,
            )
            lows = [item.astype(BF) for item in turned]
            for part in range(3):
                rows_out[base + 10 + part : base + 11 + part, lanes] = jnp.sum(
                    lows[part].astype(F32), axis=0, keepdims=True
                )
                store(side, part, dot(lows[part], normed[...], 0, 0))
            for copy in needed[side]:
                copy.wait()
            for part in range(3):
                term = dot(lows[part], held[side, part], 1, 0)
                gathered = term if gathered is None else gathered + term
        through, grad_gain, grad_shift = norm_back(inputs_kept[...].astype(F32), gain[...], gathered)
        result[...] = grad_middle[...] + through
        rows_out[base : base + 1] = grad_gain
        rows_out[base + 1 : base + 2] = grad_shift
        rows_out[base + 2 : base + 3] = sums2[2:3]
        rows_out[base + 3 : base + 5] = sums2[0:2]
        rows_out[base + 5 : base + 6] = sums2[3:4]
        rows_out[base + 6 : base + 10] = up_bias_grad[...]
        rows_out[base + 15 : base + 16] = jnp.zeros((1, rows_out.buffer.shape[1]), F32)
        for copy in leaving:
            copy.wait()

    rows = SMALL_ROWS * (len(little) - 1)
    outs = [jax.ShapeDtypeStruct((rows, width), F32), jax.ShapeDtypeStruct((count, width), F32)]
    whole = jax.ShapeDtypeStruct((4, inner, width), BF)
    part = jax.ShapeDtypeStruct((4, inner // 2, width), BF)
    ordered = [normed, incoming, places]
    for grad_query, grad_kept, came_key, came_value, query, kept, cosine, sine, mixed in sides:
        ordered += [mixed, grad_query, query, grad_kept, came_key, came_value, kept, cosine, sine]
    found = staged(
        body, "qkv_back", 32 * count * width * 2 * inner, x_bit,
        ordered + [gain, inputs_kept, grad_middle] + list(little), tuple(near) + tuple(far), outs,
        ([whole] + [part] * 2) * 2,
        (
            pltpu.VMEM((2, 4, 2 * inner, width), BF),
            pltpu.VMEM((2, 4, 2 * inner, width), BF),
            pltpu.SemaphoreType.DMA((6,)),
            pltpu.SemaphoreType.DMA((40,)),
        ),
        gates,
    )
    return (found[2], found[3:5], found[5], found[6:8]), found[:2]


def run_tasks(place, tasks, gates, alone):
    inputs = [item for task in tasks for item in task[0]]
    outs = [jax.ShapeDtypeStruct(*item) for task in tasks for item in task[1]]

    def body(at, sources, _, results, __):
        for task in tasks:
            task[2](at[0], sources[: len(task[0])], results[: len(task[1])])
            sources, results = sources[len(task[0]) :], results[len(task[1]) :]

    if alone:

        def kernel(at, *refs):
            body(at, refs[: len(inputs)], (), refs[len(inputs) + len(gates) :], ())

        found = pl.pallas_call(
            kernel,
            out_shape=outs,
            in_specs=[SCALAR] + [WHOLE] * len(inputs) + [PLACE] * len(gates),
            out_specs=[WHOLE] * len(outs),
            compiler_params=pltpu.CompilerParams(vmem_limit_bytes=24 * 2**20),
            name="sums_alone",
            cost_estimate=pl.CostEstimate(flops=0, bytes_accessed=2**20, transcendentals=0),
        )(place, *inputs, *gates)
    else:
        found = staged(body, "sums", 0, place, inputs, (), outs, gates=gates)
    given = []
    for task in tasks:
        given.append(found[: len(task[1])])
        found = found[len(task[1]) :]
    return given


def wide(ref):
    return ref[...].astype(F32)


class Piece:
    def __init__(self, swapped=False):
        self.swapped = swapped

    def begin(self, found):
        self.own, first, self.second, third = found
        self.came_near = [over_core(item) for item in first]
        self.came_far = [over_core(item) for item in third]
        return self.came_near + self.came_far

    def sources(self):
        return (self.own, self.second, *self.came_near, *self.came_far)

    def sum_of(self, sources, quarter, slot, high):
        mine = sources[quarter]
        many = (len(sources) - 2) // 2
        parts = sources[2 + many * quarter : 2 + many * (quarter + 1)]
        if mine.shape[0] == 2:
            rows = mine.shape[1] // 2
            own = mine[slot, high * rows : (high + 1) * rows]
            came = jnp.concatenate([parts[2 * high][slot], parts[2 * high + 1][slot]], axis=0)
        else:
            own = mine[2 * slot + high]
            came = jnp.concatenate([part[2 * slot + high] for part in parts], axis=0)
        return own.astype(F32) + came.astype(F32)

    def size(self):
        slots, rows, width = self.own.shape
        return slots * rows // 4, width

    def cross(self):
        half, width = self.size()

        def sums(at, sources, results):
            del at
            for slot in range(2):
                results[0][slot] = self.sum_of(sources, 1, slot, 0).astype(BF)
                results[1][slot] = self.sum_of(sources, 0, slot, 0).astype(BF)
                results[2 + slot][0] = self.sum_of(sources, 0, slot, 1).astype(BF)
                results[2 + slot][1] = self.sum_of(sources, 1, slot, 1).astype(BF)

        def after(found):
            up, self.low, self.high, away = found
            self.across, self.sideways = over_y(up), over_bit(away, 0)
            return [self.across, self.sideways]

        return self.sources(), [((2, half, width), BF)] * 4, sums, after

    def turn(self):
        _, half, width = self.low.shape

        def sums(at, sources, results):
            del at
            for way in range(2):
                results[2 * way][...] = sources[2 * way][0].astype(F32) + sources[2 * way + 1][0].astype(F32)
                results[2 * way + 1][...] = (
                    sources[2 * way][1].astype(F32) + sources[2 * way + 1][1].astype(F32)
                ).astype(BF)

        def after(found):
            self.low_kept, low, self.high_kept, high = found
            self.low_came, self.high_came = over_bit(low, 0), over_y(high)
            return [self.low_came, self.high_came]

        shapes = [((half, width), F32), ((half, width), BF)] * 2
        return (self.low, self.across, self.high, self.sideways), shapes, sums, after

    def total_parts(self):
        if self.kept is None:
            inputs = (self.low_kept, self.low_came, self.high_kept, self.high_came)
            rows, width = self.low_kept.shape

            def total(sources):
                low, high = wide(sources[0]) + wide(sources[1]), wide(sources[2]) + wide(sources[3])
                return jnp.concatenate([low, high], axis=0)

            return inputs, 2 * rows, width, total

        def total(sources):
            result = wide(sources[0])
            for source in sources[1:]:
                result = result + wide(source)
            return result

        return (self.kept,) + tuple(self.came), self.kept.shape[0], self.kept.shape[1], total

    def halve(self, bit):
        inputs, rows, width, total_of = self.total_parts()
        half = rows // 2

        def sums(at, sources, results):
            total = total_of(sources)
            low, high = total[:half], total[half:]
            first = ((at >> bit) & 1) == 0
            results[0][...] = jnp.where(first, low, high)
            results[1][...] = jnp.where(first, high, low).astype(BF)

        def after(found):
            self.kept = found[0]
            self.came = (over_bit(found[1], bit),)
            return list(self.came)

        return inputs, [((half, width), F32), ((half, width), BF)], sums, after

    def whole(self):
        inputs, rows, width, total_of = self.total_parts()

        def sums(at, sources, results):
            del at
            results[0][...] = total_of(sources).astype(BF)

        return inputs, [((rows, width), BF)], sums, self.spread

    def spread(self, found):
        self.total = found[0]
        self.others = (over_bit(self.total, self.ways.pop()),)
        return list(self.others)

    def join(self, bit):
        rows, width = self.total.shape

        def sums(at, sources, results):
            first = ((at >> bit) & 1) == 0
            mine, other = sources[0][...], sources[1][...]
            results[0][:rows] = jnp.where(first, mine, other)
            results[0][rows:] = jnp.where(first, other, mine)

        return (self.total,) + self.others, [((2 * rows, width), BF)], sums, self.spread

    def tasks(self):
        bits = lax.axis_size("dp").bit_length() - 1
        self.kept = None
        calls = [self.cross, self.turn] + [partial(self.halve, bit) for bit in range(1, bits)]
        self.ways = list(range(bits))
        if self.swapped and bits > 1:
            self.ways[:2] = [1, 0]
        calls += [self.whole] + [partial(self.join, bit) for bit in reversed(self.ways[1:])]
        return calls

    def result(self, bit):
        return (
            jnp.where(bit == 0, self.total, self.others[0]).astype(F32),
            jnp.where(bit == 0, self.others[0], self.total).astype(F32),
        )


class Whole(Piece):
    def over(self):
        half, width = self.size()

        def sums(at, sources, results):
            del at
            for slot in range(2):
                for high in range(2):
                    rows = slice(high * half, (high + 1) * half)
                    results[0][slot, rows] = self.sum_of(sources, 1, slot, high).astype(BF)
                    results[1][slot, rows] = self.sum_of(sources, 0, slot, high).astype(BF)

        def after(found):
            self.across, self.low = over_y(found[0]), found[1]
            return [self.across]

        return self.sources(), [((2, 2 * half, width), BF)] * 2, sums, after

    def along(self):
        def sums(at, sources, results):
            del at
            results[0][...] = (wide(sources[0]) + wide(sources[1])).astype(BF)

        def after(found):
            self.total = lax.psum(found[0], "dp")
            return []

        return (self.low, self.across), [(self.low.shape, BF)], sums, after

    def tasks(self):
        return [self.over, self.along]

    def result(self, bit):
        del bit
        return self.total[0].astype(F32), self.total[1].astype(F32)


class Small:
    def __init__(self, rows):
        self.mine, self.other = rows, over_core(rows)

    def add(self, quarter_bit, mine, other, result):
        rows, width = mine.shape
        lanes = width // 4
        if not quarter_bit:
            result[...] = mine[...] + other[...]
            return
        for base in range(0, rows, SMALL_ROWS):
            result[base : base + 6] = mine[base : base + 6] + other[base : base + 6]
            for quarter in range(4):
                own, partner = base + 6 + quarter, base + 6 + (quarter ^ quarter_bit)
                result[own : own + 1] = mine[own : own + 1] + other[partner : partner + 1]
            tail = other[base + 8 : base + SMALL_ROWS]
            if quarter_bit == 2:
                moved = pltpu.roll(tail, 2 * lanes, 1)
            else:
                lane = lax.broadcasted_iota(jnp.int32, tail.shape, 1)
                moved = jnp.where(
                    lane % (2 * lanes) < lanes, pltpu.roll(tail, 3 * lanes, 1), pltpu.roll(tail, lanes, 1)
                )
            result[base + 10 : base + SMALL_ROWS] = mine[base + 10 : base + SMALL_ROWS] + moved[2:]

    def step(self, quarter_bit, move):
        rows, width = self.mine.shape

        def sums(at, sources, results):
            del at
            self.add(quarter_bit, *sources, results[0])

        def after(found):
            self.mine = found[0]
            self.other = move(self.mine)
            return [self.other]

        return (self.mine, self.other), [((rows, width), F32)], sums, after

    def last(self):
        rows, width = self.mine.shape
        layers, lanes = rows // SMALL_ROWS, width // 4

        def sums(at, sources, results):
            del at
            self.add(2, *sources, results[9])
            total = results[9][...]
            for layer in range(layers):
                base = SMALL_ROWS * (layers - 1 - layer)
                for item in range(7):
                    results[item][layer : layer + 1] = total[base + item : base + item + 1]
                results[7][layer] = total[base + 10 : base + 13, :lanes]
                turned = total[base + 13 : base + 15, :lanes]
                results[8][layer] = jnp.concatenate(
                    [
                        turned[:, at : at + HALF] + turned[:, at + HALF : at + HEAD_DIM]
                        for at in range(0, lanes, HEAD_DIM)
                    ],
                    axis=1,
                )

        def after(found):
            self.found = found
            return []

        shapes = [((layers, width), F32)] * 7 + [((layers, 3, lanes), F32), ((layers, 2, lanes // 2), F32)]
        shapes.append(((rows, width), F32))
        return (self.mine, self.other), shapes, sums, after

    def tasks(self):
        bits = lax.axis_size("dp").bit_length() - 1
        moves = [partial(over_bit, bit=bit) for bit in (1, 0, *range(2, bits))] + [over_y]
        quarters = [1] + [0] * bits
        return [partial(self.step, *item) for item in zip(quarters, moves)] + [self.last]


def attention_outputs(place, pieces):
    _, width = pieces[0].total.shape
    inner = pieces[0].total.shape[0] // 2
    layers = len(pieces)

    def body(numbers, inputs, _, results, __):
        for layer in reversed(range(layers)):
            mine, other = inputs[2 * layer : 2 * layer + 2]
            ahead = ((numbers[0] >> 1) & 1) == 0
            first = jnp.where(ahead, mine[...], other[...]).astype(F32)
            second = jnp.where(ahead, other[...], mine[...]).astype(F32)
            results[0][layer, 0] = first[:inner]
            results[0][layer, 1] = second[:inner]
            results[0][layer, 2] = first[inner:]
            results[0].leave(layer)
            results[1][layer] = second[inner:]
            results[1].leave(layer)

    items = [item for piece in pieces for item in (piece.total, piece.others[0])]
    return staged(
        body, "attention_outputs", 0, place, items, (),
        (jax.ShapeDtypeStruct((layers, 3, inner, width), F32), jax.ShapeDtypeStruct((layers, inner, width), F32)),
    )


def over_bits(values, mask):
    size = lax.axis_size("dp")
    return lax.ppermute(values, "dp", [(at, at ^ mask) for at in range(size)])


def over_both(values):
    return lax.ppermute(values, "tensor", [(at, at ^ 3) for at in range(4)])


class FarFetch:
    def __init__(self, half):
        self.mine = over_y(half)

    def turn(self, hold):
        self.mine, _ = lax.optimization_barrier((self.mine, hold))
        self.other = over_bit(self.mine, 0)
        self.mine_core = over_core(self.mine)

    def end(self, hold):
        self.other, _ = lax.optimization_barrier((self.other, hold))
        self.found = (self.mine, self.other, self.mine_core, over_core(self.other))


def body(
    tokens,
    out_grad,
    image_lengths,
    norm1_gain,
    norm1_bias,
    qkv_weight,
    qkv_bias,
    rope_freqs,
    out_weight,
    out_bias,
    norm2_gain,
    norm2_bias,
    up_weight,
    up_bias,
    down_weight,
    down_bias,
):
    count, width = tokens.shape
    inner = qkv_weight.shape[3]
    heads = inner // HEAD_DIM
    me = lax.axis_index("tensor")
    xbit = lax.axis_index("dp") & 1
    x_bit = jnp.stack([xbit, xbit]).astype(jnp.int32)
    x_bit_plain = jnp.stack([xbit, jnp.zeros_like(xbit)]).astype(jnp.int32)

    small = jnp.concatenate(
        [qkv_bias.reshape(LAYERS, -1), rope_freqs.reshape(LAYERS, -1), up_bias], axis=1
    )
    near_small, far_small = (small, over_core(small)), (over_y(small), over_both(small))

    lengths = lax.dynamic_index_in_dim(image_lengths, me // 2, 0, keepdims=False)
    half_at = me % 2
    position = jnp.arange(count, dtype=jnp.int32)
    segment, row_at, column_at = places_at(lengths, position + half_at * count)
    segment_other, _, _ = places_at(lengths, position + (1 - half_at) * count)
    here_segment = segment[:, None].astype(F32)
    all_segments = jnp.concatenate([segment, segment_other])[None, :].astype(F32)
    places = jnp.stack([row_at, column_at], axis=1).astype(F32)

    qkv_turned = jnp.swapaxes(qkv_weight, 2, 3)
    near_att, far_att, near_mlp, far_mlp = [], [], [], []

    def fetch_att(layer, gates=()):
        packed, half = pack(layer, x_bit, qkv_turned, out_weight[:, None], 2, gates)
        near_att.append((packed, over_core(packed)))
        far_att.append(FarFetch(half))

    def fetch_mlp(layer, gates=()):
        both, half = pack(layer, x_bit, up_weight[:, None], down_weight[:, None], 1, gates)
        near_mlp.append((both, over_core(both)))
        far_mlp.append(FarFetch(half[0]))

    current = tokens
    kept_layers = []
    cosines, sines = [[] for _ in range(LAYERS)], [[] for _ in range(LAYERS)]
    before = ()
    fetch_att(0)
    for l in range(LAYERS):
        inputs = current
        gain, shift = norm1_gain[l : l + 1], norm1_bias[l : l + 1]
        queries, keeps, comes, mixes, spreads, exps = [], [], [], [], [], []

        def project(side, source, weights):
            nonlocal before
            found = qkv_part(
                side == 0, l, x_bit, source, gain, shift, (near_small, far_small)[side], places, weights, before
            )
            before = (found[0],)
            queries.append(found[0])
            keeps.append(found[1])
            comes.append(over_core(found[2]))
            cosines[l].append(found[3])
            sines[l].append(found[4])
            return found

        def mix(side):
            nonlocal before
            found = attend(queries[side], keeps[side], comes[side], here_segment, all_segments, x_bit, before)
            before = (found[0],)
            mixes.append(found[0])
            spreads.append(found[1])
            exps.append(found[2])

        normed = project(0, inputs, near_att[l])[5]
        if l:
            far_mlp[l].turn(queries[0])
        if l == 0:
            fetch_mlp(0, before + far_small)
            before = (near_mlp[0][0],)
            far_att[0].turn(near_mlp[0][0])
            mix(0)
            fetch_att(1, before)
            before = (near_att[1][0],)
            far_att[0].end(mixes[0])
            far_mlp[0].turn(mixes[0])
            project(1, normed, far_att[0].found)
            mix(1)
            fetch_mlp(1, before)
            before = (near_mlp[1][0],)
            far_att[1].turn(mixes[1])
            far_mlp[0].end(mixes[1])
        else:
            project(1, normed, far_att[l].found)
            mix(0)
            mix(1)
            far_mlp[l].end(mixes[1])
        middle, normed_mlp, active_near, slope_near, total = mlp_near(
            l, x_bit, inputs, mixes[0], mixes[1], out_bias[l : l + 1], norm2_gain[l : l + 1], norm2_bias[l : l + 1],
            near_small, down_bias[l : l + 1], near_att[l] + far_att[l].found, near_mlp[l], before,
        )
        active_far, slope_far, current = mlp_far(
            l, x_bit, normed_mlp, total, far_small, far_mlp[l].found, BF if l == LAYERS - 1 else F32
        )
        before = (current,)
        if l == 0:
            far_att[1].end(middle)
        kept_layers.append(
            (inputs, normed, queries, keeps, comes, mixes, spreads, exps, middle, normed_mlp, (active_near, active_far), (slope_near, slope_far))
        )
    activations = current

    gradient = out_grad
    small_rows = []
    summed = [None] * LAYERS
    waiting = []
    todo = []
    clock = 0
    latest = []
    here = lax.axis_index("dp").reshape(1).astype(jnp.int32)

    def ran(found):
        latest[:] = found[:1]
        return found

    def wait_until(arrays, when):
        waiting.append((when, arrays))

    def gates_now():
        nonlocal clock
        clock += 1
        due = [array for when, arrays in waiting if when <= clock for array in arrays]
        waiting[:] = [item for item in waiting if item[0] > clock]
        turn = [entry for entry in todo if entry[0] == clock]
        todo[:] = [entry for entry in todo if entry[0] != clock]
        if not turn:
            return due + latest
        tasks = [step() for _, _, step in turn]
        found = run_tasks(here, [task[:3] for task in tasks], due + latest, clock > 3 * LAYERS + 1)
        for (_, length, _), task, given in zip(turn, tasks, found):
            wait_until(task[3](given), clock + length)
        latest[:] = found[0][:1]
        return latest

    def plan(piece, base, table):
        start, length = 0, 1
        for at, step in enumerate(piece.tasks()):
            start, length = table[at] if at < len(table) else (start + length, 1)
            todo.append((base + start, length, step))

    for l in reversed(range(LAYERS)):
        (inputs, normed, queries, keeps, comes, mixes, spreads, exps, middle, normed_mlp, active, slope) = kept_layers[l]
        att = (near_att[l], far_att[l].found)
        pieces = [Piece(), Piece(swapped=True)]
        tables = PLANS[l > 0]
        for piece, table in zip(pieces, tables):
            plan(piece, clock, table)
        found, rest = mlp_back(
            x_bit, gradient, normed_mlp, middle, norm2_gain[l : l + 1], active, slope, near_mlp[l],
            far_mlp[l].found, gates_now(),
        )
        ran(rest)
        up_bias_grad, sums2, grad_middle, incoming = rest
        wait_until(pieces[0].begin(found), clock + tables[0][0][0] - 1)
        backs = attend_back(
            x_bit, incoming,
            [(queries[side], keeps[side], comes[side], mixes[side], spreads[side], exps[side]) for side in range(2)],
            *att, gates_now(),
        )
        ran(backs[0])
        sides = [
            (back[0], back[1], over_core(back[2]), over_core(back[3]), queries[side], keeps[side], cosines[l][side], sines[l][side], mixes[side])
            for side, back in enumerate(backs)
        ]
        found, rest = qkv_back(
            x_bit, normed, incoming, places, sides, *att, norm1_gain[l : l + 1], inputs, grad_middle,
            [sums2, up_bias_grad] + small_rows, gates_now(),
        )
        ran(rest)
        rows, gradient = rest
        small_rows = [rows]
        wait_until(pieces[1].begin(found), clock + tables[1][0][0] - 3)
        summed[l] = pieces

    little = Small(small_rows[0])
    wait_until([little.other], clock + SMALL_PLAN[0][0])
    plan(little, clock, SMALL_PLAN)
    while todo:
        gates_now()
    gain1, shift1, bias_out, gain2, shift2, bias_down, bias_up, bias_qkv, turns = little.found[:9]
    grad_qkv, grad_out = attention_outputs(here, [summed[l][1] for l in range(LAYERS)])
    grad_up, grad_down = zip(*(summed[l][0].result(xbit) for l in range(LAYERS)))
    return (
        activations,
        gradient,
        gain1,
        shift1,
        jnp.swapaxes(grad_qkv, 2, 3),
        bias_qkv,
        turns,
        grad_out,
        bias_out,
        gain2,
        shift2,
        jnp.stack(grad_up),
        bias_up,
        jnp.stack(grad_down),
        bias_down,
    )


def solution(mesh):
    in_specs = (
        P(("dp", "tensor"), None),
        P(("dp", "tensor"), None),
        P("dp", None),
        P(),
        P(),
        P(None, None, None, "tensor"),
        P(None, None, "tensor"),
        P(None, None, "tensor"),
        P(None, "tensor", None),
        P(),
        P(),
        P(),
        P(None, None, "tensor"),
        P(None, "tensor"),
        P(None, "tensor", None),
        P(),
    )
    out_specs = (
        P(("dp", "tensor"), None),
        P(("dp", "tensor"), None),
        P(),
        P(),
        P(None, None, None, "tensor"),
        P(None, None, "tensor"),
        P(None, None, "tensor"),
        P(None, "tensor", None),
        P(),
        P(),
        P(),
        P(None, None, "tensor"),
        P(None, "tensor"),
        P(None, "tensor", None),
        P(),
    )
    return jax.shard_map(body, mesh=mesh, in_specs=in_specs, out_specs=out_specs, check_vma=False)
```
